256 devices in a mesh: dp: 16 (over y, x_hi, core), fsdp: 16 (over x_lo, z).
Axes of the slice: x: 4 (x_hi: 2, x_lo: 2; x = x_hi * 2 + x_lo), y: 4, z: 8, core: 2. Of those that a mesh axis runs over, the one named last changes fastest.
Arguments:
- tokens: bfloat16 [2048, 7168], P('fsdp', 'dp'), may hold values from -6 to 6
- cotangent: bfloat16 [2048, 7168], P('fsdp', 'dp'), may hold values from -6 to 6
- gate_codes: bfloat16 [7168, 14336], P('dp', 'fsdp'), may hold values from -127 to 127
- gate_scale: float32 [14336], P('fsdp'), may hold values from 6.471994e-05 to 0.00040449965
- up_codes: bfloat16 [7168, 14336], P('dp', 'fsdp'), may hold values from -127 to 127
- up_scale: float32 [14336], P('fsdp'), may hold values from 6.471994e-05 to 0.00040449965
- down_codes: bfloat16 [14336, 7168], P('fsdp', 'dp'), may hold values from -127 to 127
- down_scale: float32 [1, 7168], P(None, 'dp'), may hold values from 4.576391e-05 to 0.00028602444
Outputs:
- output: bfloat16 [2048, 7168], P('fsdp', 'dp')
- d_tokens: bfloat16 [2048, 7168], P('fsdp', 'dp')
- grad_gate: float32 [7168, 14336], P('dp', 'fsdp')
- grad_up: float32 [7168, 14336], P('dp', 'fsdp')
- grad_down: float32 [14336, 7168], P('fsdp', 'dp')
The draws below stay inside these ranges and needn't reach their ends.
All inputs are finite; a program needn't handle non-finite values.
Results may differ from the reference program's by a relative error of at most 0.035.
Values may be sent and summed in bfloat16 or wider, within the bound.
A program may use at most 128 MiB of HBM per device.

```python
import math
import jax
import jax.numpy as jnp
from jax import lax

D = 7168
FF = 14336
TOKENS = 2048
N_DP = 16
N_FSDP = 16


def draw_gate_codes(key, part):
    key = jax.random.fold_in(key, 11)
    return jax.random.randint(key, (D, FF), -127, 128).astype(jnp.float32).astype(jnp.bfloat16)


def draw_up_codes(key, part):
    key = jax.random.fold_in(key, 23)
    return jax.random.randint(key, (D, FF), -127, 128).astype(jnp.float32).astype(jnp.bfloat16)


def draw_down_codes(key, part):
    key = jax.random.fold_in(key, 37)
    return jax.random.randint(key, (FF, D), -127, 128).astype(jnp.float32).astype(jnp.bfloat16)


def steps_of(own_key, extent, pieces, least, top_value):
    factor_of = 1.0
    for dim, parts in pieces:
        steps = jax.random.uniform(jax.random.fold_in(jax.random.fold_in(own_key, 6), dim), (parts,), jnp.float32, least / len(pieces), top_value / len(pieces))
        factor_of = factor_of * jnp.repeat(jnp.exp(steps), extent[dim] // parts).reshape((-1,) + (1,) * (len(extent) - 1 - dim))
    return factor_of


def gaussian(key, dims, width, reach, pieces=(), kind=jnp.bfloat16):
    values = width * jax.random.normal(key, dims, jnp.float32)
    if pieces:
        values = values * steps_of(key, dims, pieces, -0.22, 0.18)
    return jnp.clip(values, -reach, reach).astype(kind)


def setup_inputs(seed: int = 0) -> dict:
    streams_of = jax.random.split(jax.random.key(seed), 9)
    tokens = gaussian(streams_of[0], (TOKENS, D), 1.0, 6.0, ((0, 16), (1, 16)))
    cotangent = gaussian(streams_of[1], (TOKENS, D), 1.0, 6.0, ((0, 16), (1, 16)))
    gate_codes = draw_gate_codes(jax.random.fold_in(streams_of[8], 71), 0)
    gate_scale = jnp.clip(jnp.exp(math.log(0.00040449965) - 1.8325815 * jax.random.uniform(streams_of[3], (FF,), jnp.float32) ** steps_of(streams_of[3], (FF,), ((0, 16),), -0.2, 0.2)), 6.471994129242375e-05, 0.00040449965)
    up_codes = draw_up_codes(jax.random.fold_in(streams_of[8], 71), 0)
    up_scale = jnp.clip(jnp.exp(math.log(0.00040449965) - 1.8325815 * jax.random.uniform(streams_of[5], (FF,), jnp.float32) ** steps_of(streams_of[5], (FF,), ((0, 16),), -0.2, 0.2)), 6.471994129242375e-05, 0.00040449965)
    down_codes = draw_down_codes(jax.random.fold_in(streams_of[8], 71), 0)
    down_scale = jnp.clip(jnp.exp(math.log(0.00028602444) - 1.8325815 * jax.random.uniform(streams_of[7], (1, D), jnp.float32) ** steps_of(streams_of[7], (1, D), ((1, 16),), -0.2, 0.2)), 4.576391074806452e-05, 0.00028602444)
    return dict(tokens=tokens, cotangent=cotangent, gate_codes=gate_codes, gate_scale=gate_scale, up_codes=up_codes, up_scale=up_scale, down_codes=down_codes, down_scale=down_scale)


def dequantize(codes, scale):
    return (codes.astype(jnp.float32) * scale).astype(jnp.bfloat16)


def contract_rows(left, right):
    return lax.dot_general(left, right, (((0,), (0,)), ((), ())), preferred_element_type=jnp.float32)


def contract_last(left, right):
    return lax.dot_general(left, right, (((1,), (1,)), ((), ())), preferred_element_type=jnp.float32)


def rounded(value):
    return lax.optimization_barrier(value.astype(jnp.bfloat16)).astype(jnp.float32)


def block_sum(count, partial_fn, initial):
    def step(index, total):
        return total + rounded(partial_fn(index))
    return lax.fori_loop(0, count, step, initial)


def reference(tokens, cotangent, gate_codes, gate_scale, up_codes, up_scale, down_codes, down_scale):
    weight_gate = dequantize(gate_codes, gate_scale[None, :])
    weight_up = dequantize(up_codes, up_scale[None, :])
    weight_down = dequantize(down_codes, down_scale)
    weight_both = jnp.concatenate((weight_gate, weight_up), axis=1)
    model_block = D // N_DP
    hidden_block = FF // N_FSDP
    row_count = tokens.shape[0]

    def gate_partial(index):
        first = (index * model_block).astype(jnp.int32)
        return jnp.dot(lax.dynamic_slice_in_dim(tokens, first, model_block, 1), lax.dynamic_slice_in_dim(weight_both, first, model_block, 0), preferred_element_type=jnp.float32)

    gate_upper = block_sum(N_DP, gate_partial, jnp.zeros((row_count, 2 * FF), jnp.float32))
    gate = gate_upper[:, :FF]
    upper = gate_upper[:, FF:]
    sigmoid_gate = jax.nn.sigmoid(gate)
    activated = gate * sigmoid_gate
    hidden = (activated * upper).astype(jnp.bfloat16)

    def out_partial(index):
        first = (index * hidden_block).astype(jnp.int32)
        return jnp.dot(lax.dynamic_slice_in_dim(hidden, first, hidden_block, 1), lax.dynamic_slice_in_dim(weight_down, first, hidden_block, 0), preferred_element_type=jnp.float32)

    output = block_sum(N_FSDP, out_partial, jnp.zeros((row_count, D), jnp.float32)).astype(jnp.bfloat16)

    def back_partial(index):
        first = (index * model_block).astype(jnp.int32)
        return contract_last(lax.dynamic_slice_in_dim(cotangent, first, model_block, 1), lax.dynamic_slice_in_dim(weight_down, first, model_block, 1))

    d_hidden = block_sum(N_DP, back_partial, jnp.zeros((row_count, FF), jnp.float32))
    d_gate = (d_hidden * upper * sigmoid_gate * (1.0 + gate * (1.0 - sigmoid_gate))).astype(jnp.bfloat16)
    d_up = (d_hidden * activated).astype(jnp.bfloat16)

    def token_partial(index):
        first = (index * hidden_block).astype(jnp.int32)
        part_gate = contract_last(lax.dynamic_slice_in_dim(d_gate, first, hidden_block, 1), lax.dynamic_slice_in_dim(weight_gate, first, hidden_block, 1))
        part_up = contract_last(lax.dynamic_slice_in_dim(d_up, first, hidden_block, 1), lax.dynamic_slice_in_dim(weight_up, first, hidden_block, 1))
        return part_gate + part_up

    d_tokens = block_sum(N_FSDP, token_partial, jnp.zeros((row_count, D), jnp.float32)).astype(jnp.bfloat16)
    grad_gate = contract_rows(tokens, d_gate)
    grad_up = contract_rows(tokens, d_up)
    grad_down = contract_rows(hidden, cotangent)
    return (output, d_tokens, grad_gate, grad_up, grad_down)
```

```python
import functools

import jax
import jax.numpy as jnp
from jax import lax
from jax.experimental import pallas as pl
from jax.experimental.pallas import tpu as pltpu
from jax.sharding import PartitionSpec as P

MESH = pl.DeviceIdType.MESH
BF16 = jnp.bfloat16
F32 = jnp.float32

BLOCK = 128
UNIT = 256
UNITS = 8
WIDE = 448
HIDE = 896
FULL = 512
C = 3 * HIDE
ROW = 16
EDGE = FULL - WIDE

ORDER = (
    ("Z", 0), ("M", 0), ("C", 0), ("XL", 0), ("Z", 1), ("M", 1), ("Y1", 0), ("C", 1), ("Z", 4), ("M", 4),
    ("C", 4), ("Z", 2), ("M", 2), ("Y1", 1), ("Y2", 0), ("Z", 5), ("C", 2), ("M", 5), ("Y1", 4), ("Z", 3),
    ("C", 5), ("M", 3), ("Y1", 2), ("Z", 6), ("C", 3), ("M", 6), ("Y2", 1), ("C", 6), ("Y2", 2), ("Z", 7),
    ("Y1", 3), ("M", 7), ("X", 1), ("Y1", 6), ("C", 7), ("Y2", 3), ("Y1", 5), ("Y2", 6), ("X", 3), ("Y1", 7),
    ("X", 6), ("G1", 3), ("Y2", 7), ("X", 2), ("G1", 6), ("X", 7), ("Y2", 5), ("G2", 3), ("G1", 7), ("X", 5),
    ("G3", 3), ("G1", 2), ("G2", 7), ("G2", 6), ("G4", 3), ("K", 3), ("G2", 2), ("G1", 5), ("Y2", 4),
    ("G3", 7), ("G4", 7), ("K", 7), ("G3", 2), ("G1", 1), ("G3", 6), ("G4", 2), ("X", 4), ("G2", 5),
    ("G4", 6), ("K", 6), ("G1", 4), ("G2", 1), ("K", 2), ("X", 0), ("W", 7), ("G3", 5), ("W", 3), ("G2", 4),
    ("G1", 0), ("G4", 5), ("K", 5), ("G3", 1), ("W", 2), ("G4", 1), ("G3", 4), ("K", 1), ("G2", 0), ("W", 5),
    ("G4", 4), ("K", 4), ("W", 4), ("G3", 0), ("W", 1), ("G4", 0), ("K", 0), ("KI", 1), ("W", 0), ("W", 6),
    ("KI", 0),
)
KINDS = ("XL", "Z", "M", "C", "Y1", "Y2", "X", "G1", "G2", "G3", "G4", "W", "K", "KI")


def dot(left, right):
    return jnp.dot(left, right, preferred_element_type=F32)


def kernel(
    tokens_t, cotangent_t, gate_codes, gate_scale, up_codes, up_scale, down_codes_t, down_scale,
    output_t, d_tokens_t, grad_gate, grad_up, grad_down_t,
    own, toks, w_in, w_out, part, core_in, y_raw, y_sum, pair, pair_in, acts, outs, chain_in, first, last_in,
    z_s, z_r, c_s, c_r, y1_s, y1_r, y2_s, y2_r, x_s, x_r, gx_s, gx_r, g1_s, g1_r, g2_s, g2_r, gc_s, gc_r, k_s, k_r, f_s, f_r,
):
    dp, fs = lax.axis_index("dp"), lax.axis_index("fsdp")
    y, xh, core = dp // 4, (dp // 2) % 2, dp % 2
    xl, z = fs // 8, fs % 8

    def at(y, xh, core, xl, z):
        return (y * 4 + xh * 2 + core, xl * 8 + z)

    sibling = at(y, xh, 1 - core, xl, z)
    y_up, y_down = at((y + 1) % 4, xh, core, xl, z), at((y + 3) % 4, xh, core, xl, z)
    across = at(y, 1 - xh, core, xl, z)
    mate = at(y, xh, core, 1 - xl, z)
    z_up, z_down = at(y, xh, core, xl, (z + 1) % 8), at(y, xh, core, xl, (z + 7) % 8)

    def copy(src, dst, send, recv, device):
        return pltpu.make_async_remote_copy(
            src_ref=src, dst_ref=dst, send_sem=send, recv_sem=recv, device_id=device, device_id_type=MESH
        )

    def rows(start, size):
        return pl.ds(pl.multiple_of(start, ROW), size)

    def mine(quarter, half, size):
        return rows(core * BLOCK + ((y + quarter) % 4) * 32 + half * ROW, size)

    def z_copy(src, unit, side, device):
        return copy(src, toks.at[unit, rows(side * BLOCK, BLOCK)], z_s.at[unit, side], z_r.at[unit, side], device)

    def core_copy(i):
        return copy(part.at[i, rows((1 - core) * BLOCK, BLOCK)], core_in.at[i], c_s.at[i], c_r.at[i], sibling)

    def y_raw_copy(i, kind, quarter, half, device):
        return copy(part.at[i, mine(quarter, half, ROW)], y_raw.at[i, kind], y1_s.at[i, kind], y1_r.at[i, kind], device)

    def y_sum_copy(i, side, device):
        return copy(y_raw.at[i, side], y_sum.at[i, side], y2_s.at[i, side], y2_r.at[i, side], device)

    def pair_copy(i):
        return copy(pair.at[i, 1 - xh], pair_in.at[i], x_s.at[i], x_r.at[i], across)

    def acts_copy(i, where, send, recv, device):
        return copy(acts.at[i, where], acts.at[i, where], send, recv, device)

    def chain_copy(src, hr, way, step, device):
        return copy(src, chain_in.at[hr, way, step], k_s.at[hr, way, step], k_r.at[hr, way, step], device)

    def last_copy():
        return copy(outs.at[7, rows(0, BLOCK)], last_in, f_s.at[0], f_r.at[0], mate)

    def stage_xl(i):
        z_copy(own, 7, 0, mate).wait_recv()
        source = toks.at[7, rows(0, BLOCK)]
        z_copy(source, 4, 1, z_up).start()
        z_copy(source, 4, 0, z_down).start()

    def stage_z(i):
        p, hr = i % 4, i // 4
        low, high = toks.at[i, rows(BLOCK, BLOCK)], toks.at[i, rows(0, BLOCK)]
        z_copy(own, i, 1, z_up).wait_recv()

        @pl.when(p * 4 + hr * 2 < 10)
        def _():
            z_copy(low, i + 1, 1, z_up).start()

        @pl.when(p < 3)
        def _():
            z_copy(own, i, 0, z_down).wait_recv()

            @pl.when(p < 2)
            def _():
                z_copy(high, i + 1, 0, z_down).start()

            @pl.when(p + hr == 3)
            def _():
                z_copy(high, i + 1, 1, z_down).start()

    def stage_m(i):
        def one(k, carry):
            left = toks[i, :, pl.ds(pl.multiple_of(k // 2 * (FULL - 128), 128), FULL)]
            part[i, :, pl.ds(pl.multiple_of(k * HIDE, 128), HIDE)] = dot(left, w_in[k]).astype(BF16)
            return carry

        lax.fori_loop(0, 3, one, 0)
        core_copy(i).start()

    def stage_c(i):
        core_copy(i).wait_recv()

        def add(k, carry):
            quarter = k % 4
            here = mine(quarter, 0, 32)
            there = rows(((y + quarter) % 4) * 32, 32)
            part[i, here] = (part[i, here].astype(F32) + core_in[i, there].astype(F32)).astype(BF16)
            return carry

        lax.fori_loop(1, 4, add, 0)
        y_raw_copy(i, 0, 2, 0, y_up).start()
        y_raw_copy(i, 1, 2, 1, y_down).start()
        y_raw_copy(i, 2, 1, 1, y_up).start()
        y_raw_copy(i, 3, 3, 0, y_down).start()
        lax.fori_loop(4, 5, add, 0)

    def stage_y1(i):
        y_raw_copy(i, 0, 2, 0, y_up).wait_recv()
        y_raw[i, 0] = (y_raw[i, 0].astype(F32) + part[i, mine(1, 0, ROW)].astype(F32)).astype(BF16)
        y_sum_copy(i, 0, y_up).start()
        y_raw_copy(i, 1, 2, 1, y_down).wait_recv()
        y_raw[i, 1] = (y_raw[i, 1].astype(F32) + part[i, mine(3, 1, ROW)].astype(F32)).astype(BF16)
        y_sum_copy(i, 1, y_down).start()

    def stage_y2(i):
        y_raw_copy(i, 2, 1, 1, y_up).wait_recv()
        y_raw_copy(i, 3, 3, 0, y_down).wait_recv()
        y_sum_copy(i, 0, y_up).wait_recv()
        y_sum_copy(i, 1, y_down).wait_recv()
        for half, raw in ((0, 3), (1, 2)):
            total = part[i, mine(0, half, ROW)].astype(F32) + y_raw[i, raw].astype(F32) + y_sum[i, half].astype(F32)
            pair[i, half] = total.astype(BF16)
        pair_copy(i).start()

    def stage_x(i):
        pair_copy(i).wait_recv()
        total = pair[i, xh].astype(F32) + pair_in[i].astype(F32)
        gate, up, d_hidden = total[:, :HIDE], total[:, HIDE : 2 * HIDE], total[:, 2 * HIDE :]
        sigmoid = jax.nn.sigmoid(gate)
        activated = gate * sigmoid
        here = mine(0, xh, ROW)
        acts[i, here, pl.ds(0, HIDE)] = (activated * up).astype(BF16)
        acts[i, here, pl.ds(HIDE, HIDE)] = (d_hidden * up * sigmoid * (1.0 + gate * (1.0 - sigmoid))).astype(BF16)
        acts[i, here, pl.ds(2 * HIDE, HIDE)] = (d_hidden * activated).astype(BF16)
        acts_copy(i, here, gx_s.at[i], gx_r.at[i], across).start()

    def stage_g1(i):
        acts_copy(i, mine(0, 1 - xh, ROW), gx_s.at[i], gx_r.at[i], across).wait_recv()
        here = mine(0, 0, 32)
        acts_copy(i, here, g1_s.at[i, 0], g1_r.at[i, 0], y_up).start()
        acts_copy(i, here, g1_s.at[i, 1], g1_r.at[i, 1], y_down).start()
        acts_copy(i, here, gc_s.at[i, 0], gc_r.at[i, 0], sibling).start()

    def stage_g2(i):
        acts_copy(i, mine(3, 0, 32), g1_s.at[i, 0], g1_r.at[i, 0], y_up).wait_recv()
        acts_copy(i, mine(3, 0, ROW), g2_s.at[i, 0], g2_r.at[i, 0], y_up).start()
        acts_copy(i, mine(1, 0, 32), g1_s.at[i, 1], g1_r.at[i, 1], y_down).wait_recv()
        acts_copy(i, mine(1, 1, ROW), g2_s.at[i, 1], g2_r.at[i, 1], y_down).start()
        acts_copy(i, mine(3, 0, 32), gc_s.at[i, 1], gc_r.at[i, 1], sibling).start()
        acts_copy(i, mine(1, 0, 32), gc_s.at[i, 2], gc_r.at[i, 2], sibling).start()

    def stage_g3(i):
        acts_copy(i, mine(2, 0, ROW), g2_s.at[i, 0], g2_r.at[i, 0], y_up).wait_recv()
        acts_copy(i, mine(2, 1, ROW), g2_s.at[i, 1], g2_r.at[i, 1], y_down).wait_recv()
        acts_copy(i, mine(2, 0, 32), gc_s.at[i, 3], gc_r.at[i, 3], sibling).start()

    def stage_g4(i):
        for k, quarter in enumerate((0, 3, 1, 2)):
            there = rows((1 - core) * BLOCK + ((y + quarter) % 4) * 32, 32)
            acts_copy(i, there, gc_s.at[i, k], gc_r.at[i, k], sibling).wait_recv()
        output = dot(acts[i, :, pl.ds(0, HIDE)], w_out[0])
        d_tokens = dot(acts[i, :, pl.ds(HIDE, HIDE)], w_out[1]) + dot(acts[i, :, pl.ds(2 * HIDE, HIDE)], w_out[2])
        outs[i, :, pl.ds(0, FULL - 128)] = output[:, : FULL - 128].astype(BF16)
        outs[i, :, pl.ds(FULL - 128, 128)] = (output[:, FULL - 128 :] + d_tokens[:, :128]).astype(BF16)
        outs[i, :, pl.ds(FULL, FULL - 128)] = d_tokens[:, 128:].astype(BF16)

    def stage_w(i):
        left = toks[i, :, pl.ds(0, FULL)].T[:WIDE]
        grad_gate[...] += dot(left, acts[i, :, pl.ds(HIDE, HIDE)])
        grad_up[...] += dot(left, acts[i, :, pl.ds(2 * HIDE, HIDE)])
        left = toks[i, :, pl.ds(FULL - 128, FULL)].T[EDGE:]
        grad_down_t[...] += dot(left, acts[i, :, pl.ds(0, HIDE)])

    def stage_k(i):
        p, hr = i % 4, i // 4
        step = 3 - p
        ahead, behind = outs.at[i, rows(0, BLOCK)], outs.at[i, rows(BLOCK, BLOCK)]

        @pl.when(p == 3)
        def _():
            @pl.when(hr == 0)
            def _():
                chain_copy(behind, 0, 0, 0, z_up).start()

            @pl.when(hr == 1)
            def _():
                chain_copy(behind, 1, 1, 0, z_down).start()

        @pl.when(p < 3)
        def _():
            for way, block, device in ((0, ahead, z_up), (1, behind, z_down)):
                @pl.when((step > 1) | (hr == way))
                def _():
                    chain_copy(block, hr, way, step - 1, device).wait_recv()
                    block[...] = (block[...].astype(F32) + chain_in[hr, way, step - 1].astype(F32)).astype(BF16)

                chain_copy(block, hr, way, step, device).start()

    def stage_ki(hr):
        i = hr * 4 + 3
        block = outs.at[i, rows(0, BLOCK)]
        chain_copy(block, hr, 0, 3, z_up).wait_recv()
        chain_copy(block, hr, 1, 3, z_down).wait_recv()
        total = block[...].astype(F32) + chain_in[hr, 0, 3].astype(F32) + chain_in[hr, 1, 3].astype(F32)
        block[...] = total.astype(BF16)

        @pl.when(hr == 0)
        def _():
            first[...] = total

        @pl.when(hr == 1)
        def _():
            last_copy().start()

    barrier = pltpu.get_barrier_semaphore()
    peers = (sibling, y_up, y_down, across, mate, z_up, z_down)
    for device in peers:
        pl.semaphore_signal(barrier, inc=1, device_id=device, device_id_type=MESH)
    own[...] = jnp.concatenate((tokens_t[...], cotangent_t[...]), axis=0).T
    pl.semaphore_wait(barrier, len(peers))

    z_copy(own, 0, 1, z_up).start()
    z_copy(own, 0, 0, z_down).start()
    z_copy(own, 7, 0, mate).start()
    toks[3, rows(0, BLOCK)] = own[...]

    zeros = jnp.zeros((EDGE, HIDE), BF16)
    w_gate = (gate_codes[...].astype(F32) * gate_scale[...].reshape(1, HIDE)).astype(BF16)
    w_in[0, :WIDE] = w_gate
    w_in[0, WIDE:] = zeros
    w_out[1] = jnp.concatenate((zeros, w_gate), axis=0).T
    w_up = (up_codes[...].astype(F32) * up_scale[...].reshape(1, HIDE)).astype(BF16)
    w_in[1, :WIDE] = w_up
    w_in[1, WIDE:] = zeros
    w_out[2] = jnp.concatenate((zeros, w_up), axis=0).T
    w_down_t = (down_codes_t[...].astype(F32) * down_scale[...].reshape(WIDE, 1)).astype(BF16)
    w_in[2, :EDGE] = zeros
    w_in[2, EDGE:] = w_down_t
    w_out[0] = jnp.concatenate((w_down_t, zeros), axis=0).T
    grad_gate[...] = jnp.zeros_like(grad_gate)
    grad_up[...] = jnp.zeros_like(grad_up)
    grad_down_t[...] = jnp.zeros_like(grad_down_t)

    stages = (
        stage_xl, stage_z, stage_m, stage_c, stage_y1, stage_y2, stage_x, stage_g1, stage_g2, stage_g3, stage_g4,
        stage_w, stage_k, stage_ki,
    )

    codes = [KINDS.index(kind) * 8 + i for kind, i in ORDER]
    codes += [len(KINDS) * 8] * (-len(codes) % 4)
    words = [sum(code << (7 * k) for k, code in enumerate(codes[n : n + 4])) for n in range(0, len(codes), 4)]

    def step(k, word):
        kind, i = word // 8 % 16, word % 8
        for number, stage in enumerate(stages):
            pl.when(kind == number)(functools.partial(stage, i))
        return word // 128

    def four_steps(n, carry):
        word = jnp.int32(words[0])
        for k in range(1, len(words)):
            word = jnp.where(n == k, words[k], word)
        lax.fori_loop(0, 4, step, word)
        return carry

    lax.fori_loop(0, len(words), four_steps, 0)

    last_copy().wait_recv()
    total = (first[...] + last_in[...].astype(F32)).astype(BF16).T
    output_t[...] = total[:WIDE]
    d_tokens_t[...] = total[WIDE:]

    def sent(i, carry):
        p, hr = i % 4, i // 4
        z_copy(own, i, 1, z_up).wait_send()

        @pl.when(p < 3)
        def _():
            z_copy(own, i, 0, z_down).wait_send()

        core_copy(i).wait_send()
        for kind in range(4):
            y_raw_copy(i, kind, 0, 0, y_up).wait_send()
        for side in range(2):
            y_sum_copy(i, side, y_up).wait_send()
            acts_copy(i, mine(0, 0, 32), g1_s.at[i, side], g1_r.at[i, side], y_up).wait_send()
            acts_copy(i, mine(0, 0, ROW), g2_s.at[i, side], g2_r.at[i, side], y_up).wait_send()
        pair_copy(i).wait_send()
        acts_copy(i, mine(0, 0, ROW), gx_s.at[i], gx_r.at[i], across).wait_send()
        for k in range(4):
            acts_copy(i, mine(0, 0, 32), gc_s.at[i, k], gc_r.at[i, k], sibling).wait_send()
        for way in range(2):
            @pl.when((p > 0) | (hr == way))
            def _():
                chain_copy(own, hr, way, p, z_up).wait_send()

        return carry

    lax.fori_loop(0, UNITS, sent, 0)
    z_copy(own, 7, 0, mate).wait_send()
    last_copy().wait_send()


def local(tokens, cotangent, gate_codes, gate_scale, up_codes, up_scale, down_codes, down_scale):
    vmem = pl.BlockSpec(memory_space=pltpu.VMEM)
    dma = pltpu.SemaphoreType.DMA
    both = lambda *shape: [dma(shape), dma(shape)]
    output_t, d_tokens_t, grad_gate, grad_up, grad_down_t = pl.pallas_call(
        kernel,
        out_shape=(
            jax.ShapeDtypeStruct((WIDE, BLOCK), BF16),
            jax.ShapeDtypeStruct((WIDE, BLOCK), BF16),
            jax.ShapeDtypeStruct((WIDE, HIDE), F32),
            jax.ShapeDtypeStruct((WIDE, HIDE), F32),
            jax.ShapeDtypeStruct((WIDE, HIDE), F32),
        ),
        in_specs=[vmem] * 8,
        out_specs=(vmem,) * 5,
        scratch_shapes=[
            pltpu.VMEM((BLOCK, 2 * WIDE), BF16),
            pltpu.VMEM((UNITS, UNIT, 2 * WIDE), BF16),
            pltpu.VMEM((3, FULL, HIDE), BF16),
            pltpu.VMEM((3, HIDE, FULL), BF16),
            pltpu.VMEM((UNITS, UNIT, C), BF16),
            pltpu.VMEM((UNITS, BLOCK, C), BF16),
            pltpu.VMEM((UNITS, 4, ROW, C), BF16),
            pltpu.VMEM((UNITS, 2, ROW, C), BF16),
            pltpu.VMEM((UNITS, 2, ROW, C), BF16),
            pltpu.VMEM((UNITS, ROW, C), BF16),
            pltpu.VMEM((UNITS, UNIT, C), BF16),
            pltpu.VMEM((UNITS, UNIT, 2 * WIDE), BF16),
            pltpu.VMEM((2, 2, 4, BLOCK, 2 * WIDE), BF16),
            pltpu.VMEM((BLOCK, 2 * WIDE), F32),
            pltpu.VMEM((BLOCK, 2 * WIDE), BF16),
            *both(UNITS, 2),
            *both(UNITS),
            *both(UNITS, 4),
            *both(UNITS, 2),
            *both(UNITS),
            *both(UNITS),
            *both(UNITS, 2),
            *both(UNITS, 2),
            *both(UNITS, 4),
            *both(2, 2, 4),
            *both(1),
        ],
        compiler_params=pltpu.CompilerParams(
            collective_id=0, has_side_effects=True, vmem_limit_bytes=64 * 1024 * 1024 - 256 * 1024
        ),
    )(
        tokens.T, cotangent.T, gate_codes, gate_scale, up_codes, up_scale, down_codes.T, down_scale.reshape(WIDE)
    )
    return output_t.T, d_tokens_t.T, grad_gate, grad_up, grad_down_t.T


def solution(mesh):
    placed = (
        P("fsdp", "dp"),
        P("fsdp", "dp"),
        P("dp", "fsdp"),
        P("fsdp"),
        P("dp", "fsdp"),
        P("fsdp"),
        P("fsdp", "dp"),
        P(None, "dp"),
    )
    return jax.shard_map(
        local,
        mesh=mesh,
        in_specs=placed,
        out_specs=(
            P("fsdp", "dp"),
            P("fsdp", "dp"),
            P("dp", "fsdp"),
            P("dp", "fsdp"),
            P("fsdp", "dp"),
        ),
        check_vma=False,
    )
```

```python
import functools

import jax
import jax.numpy as jnp
from jax import lax
from jax.experimental import pallas as pl
from jax.experimental.pallas import tpu as pltpu
from jax.sharding import PartitionSpec as P

MESH = pl.DeviceIdType.MESH
BF16 = jnp.bfloat16
F32 = jnp.float32

BLOCK = 128
UNIT = 256
UNITS = 8
WIDE = 448
HIDE = 896
FULL = 512
C = 3 * HIDE
ROW = 16
HALF = 64
CUT = 11 * 128
EDGE = FULL - WIDE

ORDER = (
    ("Z", 0, 0), ("Z", 0, 1), ("M", 0, 0), ("Z", 1, 0), ("CX", 0, 0), ("Z", 1, 1), ("M", 1, 0), ("Z", 2, 0),
    ("C", 1, 0), ("Z", 2, 1), ("M", 2, 0), ("Z", 3, 0), ("XL", 0, 0), ("Y1", 1, 0), ("XL", 0, 1), ("C", 2, 0),
    ("Z", 3, 1), ("M", 3, 0), ("Z", 4, 0), ("Y2", 1, 0), ("Z", 7, 0), ("C", 3, 0), ("Y1", 2, 0), ("Z", 4, 1),
    ("M", 4, 0), ("Z", 7, 1), ("M", 7, 0), ("CX", 4, 0), ("Y1", 3, 0), ("Z", 5, 0), ("Z", 5, 1), ("C", 7, 0),
    ("M", 5, 0), ("C", 5, 0), ("Y2", 3, 0), ("Z", 6, 0), ("X", 1, 0), ("Y2", 2, 0), ("Z", 6, 1), ("Y1", 7, 0),
    ("Y1", 5, 0), ("M", 6, 0), ("XN", 3, 0), ("GA", 3, 0), ("Y2", 7, 0), ("C", 6, 0), ("X", 2, 0),
    ("G1X", 3, 0), ("Y1", 6, 0), ("XN", 7, 0), ("GA", 7, 0), ("G2X", 3, 0), ("G1", 2, 0), ("Y2", 6, 0),
    ("Y2", 5, 0), ("G1X", 7, 0), ("XA", 4, 0), ("G2", 2, 0), ("G3X", 3, 0), ("XN", 6, 0), ("G2X", 7, 0),
    ("GA", 6, 0), ("G4", 3, 0), ("K", 3, 0), ("Y1X", 4, 0), ("G3", 2, 0), ("G1", 1, 0), ("X", 5, 0),
    ("K", 3, 1), ("G1X", 6, 0), ("G4", 2, 0), ("K", 2, 0), ("G3X", 7, 0), ("G2", 1, 0), ("XX", 4, 0),
    ("XA", 0, 0), ("K", 2, 1), ("G4", 7, 0), ("SG", 3, 0), ("G1", 5, 0), ("K", 7, 0), ("G2X", 6, 0),
    ("K", 7, 1), ("G3", 1, 0), ("W", 2, 0), ("Y1X", 0, 0), ("G4", 1, 0), ("S", 2, 0), ("G2", 5, 0),
    ("K", 1, 0), ("G1", 4, 0), ("K", 1, 1), ("G3X", 6, 0), ("W", 1, 0), ("XX", 0, 0), ("G4", 6, 0),
    ("SG", 7, 0), ("K", 6, 0), ("K", 6, 1), ("G3", 5, 0), ("G2", 4, 0), ("W", 7, 0), ("G1", 0, 0),
    ("G4", 5, 0), ("S", 1, 0), ("K", 5, 0), ("G3", 4, 0), ("W", 3, 0), ("G2", 0, 0), ("K", 5, 1), ("G4", 4, 0),
    ("SG", 6, 0), ("K", 4, 0), ("G3", 0, 0), ("K", 4, 1), ("G4", 0, 0), ("S", 5, 0), ("K", 0, 0), ("KI", 1, 0),
    ("W", 5, 0), ("K", 0, 1), ("SX", 0, 0), ("SX", 4, 0), ("KI", 1, 1), ("W", 4, 0), ("W", 0, 0), ("KI", 0, 0),
    ("W", 6, 0), ("GO", 0, 0), ("KI", 0, 1),
)
KINDS = ("XL", "Z", "M", "C", "Y1", "Y2", "X", "G1", "G2", "G3", "G4", "W", "K", "KI", "S", "GO", "CX", "XA", "Y1X", "XX", "XN", "XXN", "GA", "G1X", "G2X", "G3X", "SX", "SG", "SXG")


def dot(left, right):
    return jnp.dot(left, right, preferred_element_type=F32)


def kernel(
    tokens_t, cotangent_t, gate_hbm, gate_scale, up_hbm, up_scale, down_hbm, down_scale,
    output_t, d_tokens_t, grads_hbm,
    codes, grads, load_sem, store_sem, own, toks, w_in, w_out, part, core_in, y_raw, y_sum, pair, pair_in, acts, outs, chain_in, first, last_in, side_in,
    z_s, z_r, c_s, c_r, y1_s, y1_r, y2_s, y2_r, x_s, x_r, gx_s, gx_r, g1_s, g1_r, g2_s, g2_r, gc_s, gc_r, k_s, k_r, f_s, f_r,
    a_s, a_r, b_s, b_r,
):
    dp, fs = lax.axis_index("dp"), lax.axis_index("fsdp")
    y, xh, core = dp // 4, (dp // 2) % 2, dp % 2
    xl, z = fs // 8, fs % 8

    def at(y, xh, core, xl, z):
        return (y * 4 + xh * 2 + core, xl * 8 + z)

    sibling = at(y, xh, 1 - core, xl, z)
    y_up, y_down = at((y + 1) % 4, xh, core, xl, z), at((y + 3) % 4, xh, core, xl, z)
    across = at(y, 1 - xh, core, xl, z)
    mate = at(y, xh, core, 1 - xl, z)
    z_up, z_down = at(y, xh, core, xl, (z + 1) % 8), at(y, xh, core, xl, (z + 7) % 8)

    def copy(src, dst, send, recv, device):
        return pltpu.make_async_remote_copy(
            src_ref=src, dst_ref=dst, send_sem=send, recv_sem=recv, device_id=device, device_id_type=MESH
        )

    def rows(start, size):
        return pl.ds(pl.multiple_of(start, ROW), size)

    def mine(quarter, half, size):
        return rows(core * BLOCK + ((y + quarter) % 4) * 32 + half * ROW, size)

    def z_copy(src, unit, side, half, device):
        dst = toks.at[unit, rows(side * BLOCK + half * HALF, HALF)]
        return copy(src, dst, z_s.at[unit, side, half], z_r.at[unit, side, half], device)

    def own_half(half):
        return own.at[rows(half * HALF, HALF)]

    def core_copy(i):
        return copy(part.at[i, rows((1 - core) * BLOCK, BLOCK)], core_in.at[i], c_s.at[i], c_r.at[i], sibling)

    def y_raw_copy(i, kind, quarter, half, device):
        return copy(part.at[i, mine(quarter, half, ROW)], y_raw.at[i, kind], y1_s.at[i, kind], y1_r.at[i, kind], device)

    def y_sum_copy(i, side, device):
        return copy(y_raw.at[i, side], y_sum.at[i, side], y2_s.at[i, side], y2_r.at[i, side], device)

    def pair_copy(i):
        return copy(pair.at[i, 1 - xh], pair_in.at[i], x_s.at[i], x_r.at[i], across)

    def acts_copy(i, where, send, recv, device):
        return copy(acts.at[i, where], acts.at[i, where], send, recv, device)

    def chain_copy(src, hr, way, step, half, device):
        where = (hr, way, step, half)
        return copy(src, chain_in.at[where], k_s.at[where], k_r.at[where], device)

    def last_copy(half):
        return copy(outs.at[7, rows(half * HALF, HALF)], last_in.at[half], f_s.at[half], f_r.at[half], mate)

    def stage_xl(i, half):
        z_copy(own_half(0), 7, 0, half, mate).wait_recv()
        source = toks.at[7, rows(half * HALF, HALF)]
        z_copy(source, 4, 1, half, z_up).start()
        z_copy(source, 4, 0, half, z_down).start()

    def stage_z(i, half):
        p, hr = i % 4, i // 4
        low = toks.at[i, rows(BLOCK + half * HALF, HALF)]
        high = toks.at[i, rows(half * HALF, HALF)]
        z_copy(own_half(0), i, 1, half, z_up).wait_recv()

        @pl.when(p * 4 + hr * 2 < 10)
        def _():
            z_copy(low, i + 1, 1, half, z_up).start()

        @pl.when(p < 3)
        def _():
            z_copy(own_half(0), i, 0, half, z_down).wait_recv()

            @pl.when(p < 2)
            def _():
                z_copy(high, i + 1, 0, half, z_down).start()

        @pl.when(i == 3)
        def _():
            z_copy(low, 7, 1, half, mate).start()

    def stage_m(i, half):
        for k, start in enumerate((0, 0, FULL - 128)):
            part[i, :, pl.ds(k * HIDE, HIDE)] = dot(toks[i, :, pl.ds(start, FULL)], w_in[k]).astype(BF16)
        core_copy(i).start()

    def stage_c(i, half):
        core_copy(i).wait_recv()

        def add(k, carry):
            quarter = k % 4
            here = mine(quarter, 0, 32)
            there = rows(((y + quarter) % 4) * 32, 32)
            part[i, here] = (part[i, here].astype(F32) + core_in[i, there].astype(F32)).astype(BF16)
            return carry

        lax.fori_loop(1, 4, add, 0)
        y_raw_copy(i, 0, 2, 0, y_up).start()
        y_raw_copy(i, 1, 2, 1, y_down).start()
        y_raw_copy(i, 2, 1, 1, y_up).start()
        y_raw_copy(i, 3, 3, 0, y_down).start()
        lax.fori_loop(4, 5, add, 0)

    def stage_y1(i, half):
        y_raw_copy(i, 0, 2, 0, y_up).wait_recv()
        y_raw[i, 0] = (y_raw[i, 0].astype(F32) + part[i, mine(1, 0, ROW)].astype(F32)).astype(BF16)
        y_sum_copy(i, 0, y_up).start()
        y_raw_copy(i, 1, 2, 1, y_down).wait_recv()
        y_raw[i, 1] = (y_raw[i, 1].astype(F32) + part[i, mine(3, 1, ROW)].astype(F32)).astype(BF16)
        y_sum_copy(i, 1, y_down).start()

    def stage_y2(i, half):
        y_raw_copy(i, 2, 1, 1, y_up).wait_recv()
        y_raw_copy(i, 3, 3, 0, y_down).wait_recv()
        y_sum_copy(i, 0, y_up).wait_recv()
        y_sum_copy(i, 1, y_down).wait_recv()
        for half, raw in ((0, 3), (1, 2)):
            total = part[i, mine(0, half, ROW)].astype(F32) + y_raw[i, raw].astype(F32) + y_sum[i, half].astype(F32)
            pair[i, half] = total.astype(BF16)
        pair_copy(i).start()

    def activate(i, total):
        gate, up, d_hidden = total[:, :HIDE], total[:, HIDE : 2 * HIDE], total[:, 2 * HIDE :]
        sigmoid = jax.nn.sigmoid(gate)
        activated = gate * sigmoid
        here = mine(0, xh, ROW)
        acts[i, here, pl.ds(0, HIDE)] = (activated * up).astype(BF16)
        acts[i, here, pl.ds(HIDE, HIDE)] = (d_hidden * up * sigmoid * (1.0 + gate * (1.0 - sigmoid))).astype(BF16)
        acts[i, here, pl.ds(2 * HIDE, HIDE)] = (d_hidden * activated).astype(BF16)

    def stage_xn(i, half):
        pair_copy(i).wait_recv()
        activate(i, pair[i, xh].astype(F32) + pair_in[i].astype(F32))

    def stage_x(i, half):
        stage_xn(i, half)
        acts_copy(i, mine(0, xh, ROW), gx_s.at[i], gx_r.at[i], across).start()

    cols = (pl.ds(0, CUT), pl.ds(CUT, C - CUT))

    def side_copy(i, k):
        return copy(part.at[i, mine(k, 1 - xh, ROW)], side_in.at[i, k], a_s.at[i, k], a_r.at[i, k], across)

    def raw_cols(i, kind, quarter, cut, device):
        where = cols[cut]
        source = part.at[i, mine(quarter, xh, ROW), where]
        return copy(source, y_raw.at[i, kind, :, where], y1_s.at[i, kind], y1_r.at[i, kind], device)

    def sum_cols(i, cut, device):
        where = cols[cut]
        return copy(y_raw.at[i, cut, :, where], y_sum.at[i, cut, :, where], y2_s.at[i, cut], y2_r.at[i, cut], device)

    def stage_cx(i, half):
        core_copy(i).wait_recv()

        def add(k, carry):
            here = mine(k, 0, 32)
            there = rows(((y + k) % 4) * 32, 32)
            part[i, here] = (part[i, here].astype(F32) + core_in[i, there].astype(F32)).astype(BF16)
            side_copy(i, k % 4).start()
            return carry

        lax.fori_loop(2, 6, add, 0)

    def stage_xa(i, half):
        for k in (2, 3, 1, 0):
            side_copy(i, k).wait_recv()
            here = mine(k, xh, ROW)
            part[i, here] = (part[i, here].astype(F32) + side_in[i, k].astype(F32)).astype(BF16)
            if k == 2:
                raw_cols(i, 0, 2, 0, y_up).start()
                raw_cols(i, 1, 2, 1, y_down).start()
            if k == 3:
                raw_cols(i, 3, 3, 0, y_down).start()
            if k == 1:
                raw_cols(i, 2, 1, 1, y_up).start()

    def stage_y1x(i, half):
        for cut, quarter, device in ((0, 1, y_up), (1, 3, y_down)):
            raw_cols(i, cut, 2, cut, device).wait_recv()
            where = cols[cut]
            term = part[i, mine(quarter, xh, ROW), where].astype(F32)
            y_raw[i, cut, :, where] = (y_raw[i, cut, :, where].astype(F32) + term).astype(BF16)
            sum_cols(i, cut, device).start()

    def stage_xxn(i, half):
        raw_cols(i, 2, 1, 1, y_up).wait_recv()
        raw_cols(i, 3, 3, 0, y_down).wait_recv()
        terms = []
        for cut, raw, device in ((0, 3, y_up), (1, 2, y_down)):
            sum_cols(i, cut, device).wait_recv()
            where = cols[cut]
            terms.append(
                part[i, mine(0, xh, ROW), where].astype(F32)
                + y_raw[i, raw, :, where].astype(F32)
                + y_sum[i, cut, :, where].astype(F32)
            )
        activate(i, jnp.concatenate(terms, axis=1))

    def stage_xx(i, half):
        stage_xxn(i, half)
        acts_copy(i, mine(0, xh, ROW), gx_s.at[i], gx_r.at[i], across).start()

    def g1_cols(i, way, part_no, quarter, device):
        where = (i, mine(quarter, xh, ROW), cols[way ^ part_no])
        return copy(acts.at[where], acts.at[where], g1_s.at[i, way, part_no], g1_r.at[i, way, part_no], device)

    def g2_cols(i, way, quarter, device):
        where = (i, mine(quarter, xh, ROW), cols[way])
        return copy(acts.at[where], acts.at[where], g2_s.at[i, way], g2_r.at[i, way], device)

    def ga_copy(i, k, half):
        return acts_copy(i, mine((0, 3, 1, 2)[k], half, ROW), b_s.at[i, k], b_r.at[i, k], across)

    def stage_ga(i, half):
        for n in range(2):
            g1_cols(i, 0, n, 0, y_up).start()
            g1_cols(i, 1, n, 0, y_down).start()
        ga_copy(i, 0, xh).start()

    def stage_g1x(i, half):
        g1_cols(i, 0, 0, 3, y_up).wait_recv()
        g2_cols(i, 0, 3, y_up).start()
        g1_cols(i, 1, 0, 1, y_down).wait_recv()
        g2_cols(i, 1, 1, y_down).start()
        g1_cols(i, 0, 1, 3, y_up).wait_recv()
        ga_copy(i, 1, xh).start()
        g1_cols(i, 1, 1, 1, y_down).wait_recv()
        ga_copy(i, 2, xh).start()

    def stage_g2x(i, half):
        g2_cols(i, 0, 2, y_up).wait_recv()
        g2_cols(i, 1, 2, y_down).wait_recv()
        ga_copy(i, 3, xh).start()

    def stage_g3x(i, half):
        for k, quarter in enumerate((0, 3, 1, 2)):
            ga_copy(i, k, 1 - xh).wait_recv()
            acts_copy(i, mine(quarter, 0, 32), gc_s.at[i, k], gc_r.at[i, k], sibling).start()

    def g1_copy(i, way, part_no, where, device):
        return acts_copy(i, where, g1_s.at[i, way, part_no], g1_r.at[i, way, part_no], device)

    def stage_g1(i, half):
        acts_copy(i, mine(0, 1 - xh, ROW), gx_s.at[i], gx_r.at[i], across).wait_recv()
        g1_copy(i, 0, 0, mine(0, 0, ROW), y_up).start()
        g1_copy(i, 1, 0, mine(0, 1, ROW), y_down).start()
        g1_copy(i, 0, 1, mine(0, 1, ROW), y_up).start()
        g1_copy(i, 1, 1, mine(0, 0, ROW), y_down).start()
        acts_copy(i, mine(0, 0, 32), gc_s.at[i, 0], gc_r.at[i, 0], sibling).start()

    def stage_g2(i, half):
        g1_copy(i, 0, 0, mine(3, 0, ROW), y_up).wait_recv()
        acts_copy(i, mine(3, 0, ROW), g2_s.at[i, 0], g2_r.at[i, 0], y_up).start()
        g1_copy(i, 1, 0, mine(1, 1, ROW), y_down).wait_recv()
        acts_copy(i, mine(1, 1, ROW), g2_s.at[i, 1], g2_r.at[i, 1], y_down).start()

    def stage_g3(i, half):
        g1_copy(i, 0, 1, mine(3, 1, ROW), y_up).wait_recv()
        acts_copy(i, mine(3, 0, 32), gc_s.at[i, 1], gc_r.at[i, 1], sibling).start()
        g1_copy(i, 1, 1, mine(1, 0, ROW), y_down).wait_recv()
        acts_copy(i, mine(1, 0, 32), gc_s.at[i, 2], gc_r.at[i, 2], sibling).start()
        acts_copy(i, mine(2, 0, ROW), g2_s.at[i, 0], g2_r.at[i, 0], y_up).wait_recv()
        acts_copy(i, mine(2, 1, ROW), g2_s.at[i, 1], g2_r.at[i, 1], y_down).wait_recv()
        acts_copy(i, mine(2, 0, 32), gc_s.at[i, 3], gc_r.at[i, 3], sibling).start()

    def stage_g4(i, half):
        for k, quarter in enumerate((0, 3, 1, 2)):
            there = rows((1 - core) * BLOCK + ((y + quarter) % 4) * 32, 32)
            acts_copy(i, there, gc_s.at[i, k], gc_r.at[i, k], sibling).wait_recv()
        output = dot(acts[i, :, pl.ds(0, HIDE)], w_out[0])
        d_tokens = dot(acts[i, :, pl.ds(HIDE, HIDE)], w_out[1]) + dot(acts[i, :, pl.ds(2 * HIDE, HIDE)], w_out[2])
        outs[i, :, pl.ds(0, FULL - 128)] = output[:, : FULL - 128].astype(BF16)
        outs[i, :, pl.ds(FULL - 128, 128)] = (output[:, FULL - 128 :] + d_tokens[:, :128]).astype(BF16)
        outs[i, :, pl.ds(FULL, FULL - 128)] = d_tokens[:, 128:].astype(BF16)

    def stage_w(i, half):
        left = toks[i, :, pl.ds(0, FULL)].T[:WIDE]
        grads[0] += dot(left, acts[i, :, pl.ds(HIDE, HIDE)])
        grads[1] += dot(left, acts[i, :, pl.ds(2 * HIDE, HIDE)])
        left = toks[i, :, pl.ds(FULL - 128, FULL)].T[EDGE:]
        grads[2] += dot(left, acts[i, :, pl.ds(0, HIDE)])

    def stage_k(i, half):
        p, hr = i % 4, i // 4
        step = 3 - p
        ahead, behind = outs.at[i, rows(half * HALF, HALF)], outs.at[i, rows(BLOCK + half * HALF, HALF)]

        @pl.when(p == 3)
        def _():
            @pl.when(hr == 0)
            def _():
                chain_copy(behind, 0, 0, 0, half, z_up).start()

            @pl.when(hr == 1)
            def _():
                chain_copy(behind, 1, 1, 0, half, z_down).start()

        @pl.when(p < 3)
        def _():
            for way, block, device in ((0, ahead, z_up), (1, behind, z_down)):
                @pl.when((step > 1) | (hr == way))
                def _():
                    chain_copy(block, hr, way, step - 1, half, device).wait_recv()
                    block[...] = (block[...].astype(F32) + chain_in[hr, way, step - 1, half].astype(F32)).astype(BF16)

                chain_copy(block, hr, way, step, half, device).start()

    def stage_ki(hr, half):
        here = rows(half * HALF, HALF)
        block = outs.at[hr * 4 + 3, here]
        chain_copy(block, hr, 0, 3, half, z_up).wait_recv()
        chain_copy(block, hr, 1, 3, half, z_down).wait_recv()
        total = block[...].astype(F32) + chain_in[hr, 0, 3, half].astype(F32) + chain_in[hr, 1, 3, half].astype(F32)
        block[...] = total.astype(BF16)

        @pl.when(hr == 0)
        def _():
            first[here] = total

        @pl.when(hr == 1)
        def _():
            last_copy(half).start()

    def sends_of(by_side, by_ring):
        def stage(i, half):
            p = i % 4
            for n in range(2):
                z_copy(own_half(0), i, 1, n, z_up).wait_send()

                @pl.when(p < 3)
                def _():
                    z_copy(own_half(0), i, 0, n, z_down).wait_send()

            core_copy(i).wait_send()
            for way in range(2):
                if by_side:
                    raw_cols(i, way, 2, way, y_up).wait_send()
                    raw_cols(i, 3 - way, 2, way, y_up).wait_send()
                    sum_cols(i, way, y_up).wait_send()
                else:
                    y_raw_copy(i, way, 0, 0, y_up).wait_send()
                    y_raw_copy(i, 3 - way, 0, 0, y_up).wait_send()
                    y_sum_copy(i, way, y_up).wait_send()
                for n in range(2):
                    if by_ring:
                        g1_cols(i, way, n, 0, y_up).wait_send()
                    else:
                        g1_copy(i, way, n, mine(0, 0, ROW), y_up).wait_send()
                if by_ring:
                    g2_cols(i, way, 0, y_up).wait_send()
                else:
                    acts_copy(i, mine(0, 0, ROW), g2_s.at[i, way], g2_r.at[i, way], y_up).wait_send()
            if by_side:
                for k in range(4):
                    side_copy(i, k).wait_send()
            else:
                pair_copy(i).wait_send()
            if by_ring:
                for k in range(4):
                    ga_copy(i, k, xh).wait_send()
            else:
                acts_copy(i, mine(0, 0, ROW), gx_s.at[i], gx_r.at[i], across).wait_send()
            for k in range(4):
                acts_copy(i, mine(0, 0, 32), gc_s.at[i, k], gc_r.at[i, k], sibling).wait_send()

        return stage

    def store(k):
        return pltpu.make_async_copy(grads.at[k], grads_hbm.at[k], store_sem.at[k])

    def stage_go(i, half):
        @pl.when(i == 0)
        def _():
            for k in range(3):
                store(k).start()

    loads = [
        pltpu.make_async_copy(ref, codes.at[k], load_sem.at[k]) for k, ref in enumerate((gate_hbm, up_hbm, down_hbm))
    ]
    for load in loads:
        load.start()
    barrier = pltpu.get_barrier_semaphore()
    peers = (sibling, y_up, y_down, across, mate, z_up, z_down)
    for device in peers:
        pl.semaphore_signal(barrier, inc=1, device_id=device, device_id_type=MESH)
    own[...] = jnp.concatenate((tokens_t[...], cotangent_t[...]), axis=0).T
    pl.semaphore_wait(barrier, len(peers))

    for half in range(2):
        z_copy(own_half(half), 0, 1, half, z_up).start()
        z_copy(own_half(half), 0, 0, half, z_down).start()
        z_copy(own_half(half), 7, 0, half, mate).start()
    toks[3, rows(0, BLOCK)] = own[...]

    zeros = jnp.zeros((EDGE, HIDE), BF16)
    grads[...] = jnp.zeros_like(grads)
    loads[0].wait()
    w_gate = (codes[0].astype(F32) * gate_scale[...].reshape(1, HIDE)).astype(BF16)
    w_in[0, :WIDE] = w_gate
    w_in[0, WIDE:] = zeros
    w_out[1] = jnp.concatenate((zeros, w_gate), axis=0).T
    loads[1].wait()
    w_up = (codes[1].astype(F32) * up_scale[...].reshape(1, HIDE)).astype(BF16)
    w_in[1, :WIDE] = w_up
    w_in[1, WIDE:] = zeros
    w_out[2] = jnp.concatenate((zeros, w_up), axis=0).T
    loads[2].wait()
    w_down_t = (codes[2].astype(F32) * down_scale[...].reshape(WIDE, 1)).astype(BF16)
    w_in[2, :EDGE] = zeros
    w_in[2, EDGE:] = w_down_t
    w_out[0] = jnp.concatenate((w_down_t, zeros), axis=0).T

    stages = (
        stage_xl, stage_z, stage_m, stage_c, stage_y1, stage_y2, stage_x, stage_g1, stage_g2, stage_g3, stage_g4,
        stage_w, stage_k, stage_ki, sends_of(False, False), stage_go, stage_cx, stage_xa, stage_y1x, stage_xx, stage_xn,
        stage_xxn, stage_ga, stage_g1x, stage_g2x, stage_g3x, sends_of(True, False), sends_of(False, True),
        sends_of(True, True),
    )

    steps = [KINDS.index(kind) * 16 + half * 8 + i for kind, i, half in ORDER]
    steps += [KINDS.index("GO") * 16 + 1] * (-len(steps) % 3)
    words = [sum(code << (9 * k) for k, code in enumerate(steps[n : n + 3])) for n in range(0, len(steps), 3)]
    groups = [stages[n : n + 4] for n in range(0, len(stages), 4)]

    def step(k, word):
        kind, half, i = word // 16 % 32, word // 8 % 2, word % 8
        for n, group in enumerate(groups):
            @pl.when(kind // 4 == n)
            def _():
                for number, stage in enumerate(group):
                    pl.when(kind % 4 == number)(functools.partial(stage, i, half))

        return word // 512

    def three_steps(n, carry):
        word = jnp.int32(words[0])
        for k in range(1, len(words)):
            word = jnp.where(n == k, words[k], word)
        lax.fori_loop(0, 3, step, word)
        return carry

    lax.fori_loop(0, len(words), three_steps, 0)

    for half in range(2):
        last_copy(half).wait_recv()
    total = (first[...] + last_in[...].reshape(BLOCK, 2 * WIDE).astype(F32)).astype(BF16).T
    output_t[...] = total[:WIDE]
    d_tokens_t[...] = total[WIDE:]

    for hr in range(2):
        for way in range(2):
            for n in range(4):
                for half in range(2):
                    if n > 0 or hr == way:
                        chain_copy(own_half(0), hr, way, n, half, z_up).wait_send()
    for half in range(2):
        z_copy(own_half(0), 7, 0, half, mate).wait_send()
        last_copy(half).wait_send()
    for k in range(3):
        store(k).wait()


def settle(*refs):
    ins, outs, held, sems = refs[:3], refs[3:8], refs[8:13], refs[13:]
    sources = [*ins[:2], *(ins[2].at[k] for k in range(3))]
    loads = [pltpu.make_async_copy(a, b, sems[0].at[k]) for k, (a, b) in enumerate(zip(sources, held))]
    stores = [pltpu.make_async_copy(a, b, sems[1].at[k]) for k, (a, b) in enumerate(zip(held, outs))]
    for one in loads:
        one.start()
    for load, one in zip(loads, stores):
        load.wait()
        one.start()
    for one in stores:
        one.wait()


def local(tokens, cotangent, gate_codes, gate_scale, up_codes, up_scale, down_codes, down_scale):
    vmem = pl.BlockSpec(memory_space=pltpu.VMEM)
    dma = pltpu.SemaphoreType.DMA
    both = lambda *shape: [dma(shape), dma(shape)]
    anywhere = pl.BlockSpec(memory_space=pl.ANY)
    edge = jax.ShapeDtypeStruct((WIDE, BLOCK), BF16)
    results = pl.pallas_call(
        kernel,
        out_shape=(edge, edge, jax.ShapeDtypeStruct((3, WIDE, HIDE), F32)),
        in_specs=[vmem, vmem, anywhere, vmem, anywhere, vmem, anywhere, vmem],
        out_specs=(vmem, vmem, anywhere),
        scratch_shapes=[
            pltpu.VMEM((3, WIDE, HIDE), BF16),
            pltpu.VMEM((3, WIDE, HIDE), F32),
            dma((3,)),
            dma((3,)),
            pltpu.VMEM((BLOCK, 2 * WIDE), BF16),
            pltpu.VMEM((UNITS, UNIT, 2 * WIDE), BF16),
            pltpu.VMEM((3, FULL, HIDE), BF16),
            pltpu.VMEM((3, HIDE, FULL), BF16),
            pltpu.VMEM((UNITS, UNIT, C), BF16),
            pltpu.VMEM((UNITS, BLOCK, C), BF16),
            pltpu.VMEM((UNITS, 4, ROW, C), BF16),
            pltpu.VMEM((UNITS, 2, ROW, C), BF16),
            pltpu.VMEM((UNITS, 2, ROW, C), BF16),
            pltpu.VMEM((UNITS, ROW, C), BF16),
            pltpu.VMEM((UNITS, UNIT, C), BF16),
            pltpu.VMEM((UNITS, UNIT, 2 * WIDE), BF16),
            pltpu.VMEM((2, 2, 4, 2, HALF, 2 * WIDE), BF16),
            pltpu.VMEM((BLOCK, 2 * WIDE), F32),
            pltpu.VMEM((2, HALF, 2 * WIDE), BF16),
            pltpu.VMEM((UNITS, 4, ROW, C), BF16),
            *both(UNITS, 2, 2),
            *both(UNITS),
            *both(UNITS, 4),
            *both(UNITS, 2),
            *both(UNITS),
            *both(UNITS),
            *both(UNITS, 2, 2),
            *both(UNITS, 2),
            *both(UNITS, 4),
            *both(2, 2, 4, 2),
            *both(2),
            *both(UNITS, 4),
            *both(UNITS, 4),
        ],
        compiler_params=pltpu.CompilerParams(
            collective_id=0, has_side_effects=True, vmem_limit_bytes=64 * 1024 * 1024 - 256 * 1024
        ),
    )(
        tokens.T, cotangent.T, gate_codes, gate_scale, up_codes, up_scale, down_codes.T, down_scale.reshape(WIDE)
    )
    grad = jax.ShapeDtypeStruct((WIDE, HIDE), F32)
    output_t, d_tokens_t, grad_gate, grad_up, grad_down_t = pl.pallas_call(
        settle,
        out_shape=(edge, edge, grad, grad, grad),
        in_specs=[anywhere] * 3,
        out_specs=(anywhere,) * 5,
        scratch_shapes=[pltpu.VMEM((WIDE, BLOCK), BF16)] * 2 + [pltpu.VMEM((WIDE, HIDE), F32)] * 3 + [dma((5,))] * 2,
        compiler_params=pltpu.CompilerParams(vmem_limit_bytes=60 * 1024 * 1024),
    )(*results)
    return output_t.T, d_tokens_t.T, grad_gate, grad_up, grad_down_t.T


def solution(mesh):
    placed = (
        P("fsdp", "dp"),
        P("fsdp", "dp"),
        P("dp", "fsdp"),
        P("fsdp"),
        P("dp", "fsdp"),
        P("fsdp"),
        P("fsdp", "dp"),
        P(None, "dp"),
    )
    return jax.shard_map(
        local,
        mesh=mesh,
        in_specs=placed,
        out_specs=(
            P("fsdp", "dp"),
            P("fsdp", "dp"),
            P("dp", "fsdp"),
            P("dp", "fsdp"),
            P("fsdp", "dp"),
        ),
        check_vma=False,
    )
```

```python
import functools

import jax
import jax.numpy as jnp
from jax import lax
from jax.experimental import pallas as pl
from jax.experimental.pallas import tpu as pltpu
from jax.sharding import PartitionSpec as P

MESH = pl.DeviceIdType.MESH
BF16 = jnp.bfloat16
F32 = jnp.float32

BLOCK = 128
UNIT = 256
UNITS = 8
WIDE = 448
HIDE = 896
FULL = 512
C = 3 * HIDE
ROW = 16
Z_PARTS = 4
Z_ROWS = BLOCK // Z_PARTS
CHAIN_PARTS = 2
CHAIN_ROWS = BLOCK // CHAIN_PARTS
CUT = 11 * 128
EDGE = FULL - WIDE

ORDER = (
    ("Z", 0, 0), ("Z", 0, 1), ("Z", 0, 2), ("Z", 0, 3), ("M", 0, 0), ("Z", 1, 0), ("Z", 1, 1), ("Z", 1, 2),
    ("CX", 0, 0), ("Z", 1, 3), ("M", 1, 0), ("Z", 2, 0), ("Z", 2, 1), ("Z", 2, 2), ("C", 1, 0), ("Z", 2, 3),
    ("XL", 0, 0), ("M", 2, 0), ("Z", 3, 0), ("Z", 3, 1), ("Y1", 1, 0), ("Z", 3, 2), ("XL", 0, 1), ("XL", 0, 2),
    ("C", 2, 0), ("Z", 3, 3), ("M", 3, 0), ("XL", 0, 3), ("Z", 4, 0), ("Z", 7, 0), ("Y2", 1, 0), ("Z", 4, 1),
    ("Z", 4, 2), ("C", 3, 0), ("Z", 7, 1), ("Z", 7, 2), ("Z", 4, 3), ("M", 4, 0), ("Z", 7, 3), ("XA", 0, 0),
    ("Z", 5, 0), ("M", 7, 0), ("Z", 5, 1), ("Y1", 3, 0), ("CX", 4, 0), ("Z", 5, 2), ("Z", 5, 3), ("Z", 6, 0),
    ("C", 7, 0), ("Z", 6, 1), ("Y1", 2, 0), ("Z", 6, 2), ("Z", 6, 3), ("M", 6, 0), ("Y2", 3, 0), ("Y1", 7, 0),
    ("C", 6, 0), ("Y2", 2, 0), ("Y2", 7, 0), ("XN", 3, 0), ("GA", 3, 0), ("M", 5, 0), ("Y1", 6, 0),
    ("X", 1, 0), ("G1X", 3, 0), ("X", 2, 0), ("C", 5, 0), ("XN", 7, 0), ("Y2", 6, 0), ("G2X", 3, 0),
    ("GA", 7, 0), ("Y1", 5, 0), ("G1X", 7, 0), ("G1", 2, 0), ("XN", 6, 0), ("Y2", 5, 0), ("G3X", 3, 0),
    ("G2X", 7, 0), ("G2", 2, 0), ("GA", 6, 0), ("G4", 3, 0), ("XA", 4, 0), ("K", 3, 0), ("K", 3, 1),
    ("G3", 2, 0), ("X", 5, 0), ("G1X", 6, 0), ("G1", 1, 0), ("G4", 2, 0), ("K", 2, 0), ("G2X", 6, 0),
    ("G3X", 7, 0), ("G2", 1, 0), ("K", 2, 1), ("Y1X", 4, 0), ("G4", 7, 0), ("Y1X", 0, 0), ("K", 7, 0),
    ("G1", 5, 0), ("G3", 1, 0), ("K", 7, 1), ("XX", 4, 0), ("W", 3, 0), ("G4", 1, 0), ("K", 1, 0),
    ("G2", 5, 0), ("G3X", 6, 0), ("XX", 0, 0), ("G1", 4, 0), ("K", 1, 1), ("G4", 6, 0), ("K", 6, 0),
    ("G3", 5, 0), ("G2", 4, 0), ("K", 6, 1), ("W", 1, 0), ("G1", 0, 0), ("G4", 5, 0), ("K", 5, 0),
    ("G3", 4, 0), ("W", 5, 0), ("G2", 0, 0), ("K", 5, 1), ("G4", 4, 0), ("K", 4, 0), ("G3", 0, 0), ("K", 4, 1),
    ("W", 7, 0), ("G4", 0, 0), ("KI", 1, 0), ("K", 0, 0), ("K", 0, 1), ("KI", 1, 1), ("W", 6, 0), ("W", 2, 0),
    ("W", 4, 0), ("W", 0, 0), ("GO", 0, 0), ("S", 7, 0), ("S", 6, 0), ("S", 5, 0), ("S", 4, 0), ("S", 3, 0),
    ("S", 2, 0), ("S", 1, 0), ("S", 0, 0), ("KI", 0, 0), ("KI", 0, 1),
)
KINDS = ("XL", "Z", "M", "C", "Y1", "Y2", "X", "G1", "G2", "G3", "G4", "W", "K", "KI", "S", "GO", "CX", "XA", "Y1X", "XX", "XN", "XXN", "GA", "G1X", "G2X", "G3X")


def dot(left, right):
    return jnp.dot(left, right, preferred_element_type=F32)


def kernel(
    tokens_hbm, cotangent_hbm, gate_hbm, gate_scale, up_hbm, up_scale, down_hbm, down_scale,
    output_t, d_tokens_t, grads_hbm,
    features_t, codes, grads, load_sem, store_sem, own, toks, w_in, w_out, part, core_in, y_raw, y_sum, pair, pair_in, acts, outs, chain_in, first, last_in, side_in,
    z_s, dp_s, k_s, f_s,
    z_r, xl_r, c_r, y1_r, y2_r, x_r, gx_r, g1_r, g2_r, gc_r, k_r, f_r,
):
    dp, fs = lax.axis_index("dp"), lax.axis_index("fsdp")
    y, xh, core = dp // 4, (dp // 2) % 2, dp % 2
    xl, z = fs // 8, fs % 8

    def at(y, xh, core, xl, z):
        return (y * 4 + xh * 2 + core, xl * 8 + z)

    sibling = at(y, xh, 1 - core, xl, z)
    y_up, y_down = at((y + 1) % 4, xh, core, xl, z), at((y + 3) % 4, xh, core, xl, z)
    across = at(y, 1 - xh, core, xl, z)
    mate = at(y, xh, core, 1 - xl, z)
    z_up, z_down = at(y, xh, core, xl, (z + 1) % 8), at(y, xh, core, xl, (z + 7) % 8)

    def copy(src, dst, send, recv, device):
        return pltpu.make_async_remote_copy(
            src_ref=src, dst_ref=dst, send_sem=send, recv_sem=recv, device_id=device, device_id_type=MESH
        )

    def rows(start, size):
        return pl.ds(pl.multiple_of(start, ROW), size)

    def mine(quarter, half, size):
        return rows(core * BLOCK + ((y + quarter) % 4) * 32 + half * ROW, size)

    def await_bytes(ref, semaphore):
        pltpu.make_async_copy(ref, ref, semaphore).wait()

    def wide_rows(count):
        return core_in.at[rows(0, count)]

    def z_copy(src, unit, side, half, device):
        dst = toks.at[unit, rows(side * BLOCK + half * Z_ROWS, Z_ROWS)]
        return copy(src, dst, z_s.at[unit], z_r.at[unit, half], device)

    def xl_copy(half):
        return copy(own_half(half), toks.at[7, rows(half * Z_ROWS, Z_ROWS)], z_s.at[7], xl_r.at[half], mate)

    def own_half(half):
        return own.at[rows(half * Z_ROWS, Z_ROWS)]

    def core_copy(i):
        source = part.at[i, rows((1 - core) * BLOCK, BLOCK)]
        return copy(source, core_in.at[rows(i * BLOCK, BLOCK)], dp_s.at[i], c_r.at[i], sibling)

    def y_raw_copy(i, kind, quarter, half, device):
        landed = (y1_r if kind < 2 else y2_r).at[i]
        return copy(part.at[i, mine(quarter, half, ROW)], y_raw.at[i, kind], dp_s.at[i], landed, device)

    def y_sum_copy(i, side, device):
        return copy(y_raw.at[i, side], y_sum.at[i, side], dp_s.at[i], y2_r.at[i], device)

    def pair_copy(i):
        return copy(pair.at[i, 1 - xh], pair_in.at[i], dp_s.at[i], x_r.at[i], across)

    def acts_copy(i, where, landed, device):
        return copy(acts.at[i, where], acts.at[i, where], dp_s.at[i], landed.at[i], device)

    def chain_copy(src, hr, way, step, half, device):
        return copy(src, chain_in.at[hr, way, step, half], k_s.at[0], k_r.at[hr, step, half], device)

    def last_copy(half):
        return copy(outs.at[7, rows(half * CHAIN_ROWS, CHAIN_ROWS)], last_in.at[half], f_s.at[0], f_r.at[0], mate)

    def stage_xl(i, half):
        xl_copy(half).wait_recv()
        source = toks.at[7, rows(half * Z_ROWS, Z_ROWS)]
        z_copy(source, 4, 1, half, z_up).start()
        z_copy(source, 4, 0, half, z_down).start()

    def stage_z(i, half):
        p, hr = i % 4, i // 4
        low = toks.at[i, rows(BLOCK + half * Z_ROWS, Z_ROWS)]
        high = toks.at[i, rows(half * Z_ROWS, Z_ROWS)]

        @pl.when(p < 3)
        def _():
            await_bytes(toks.at[i, rows(0, 2 * Z_ROWS)], z_r.at[i, half])

        @pl.when(p == 3)
        def _():
            await_bytes(toks.at[i, rows(BLOCK, Z_ROWS)], z_r.at[i, half])

        @pl.when(p * 4 + hr * 2 < 10)
        def _():
            z_copy(low, i + 1, 1, half, z_up).start()

        @pl.when(p < 2)
        def _():
            z_copy(high, i + 1, 0, half, z_down).start()

        @pl.when(i == 3)
        def _():
            z_copy(low, 7, 1, half, mate).start()

    def stage_m(i, half):
        for k, start in enumerate((0, 0, FULL - 128)):
            part[i, :, pl.ds(k * HIDE, HIDE)] = dot(toks[i, :, pl.ds(start, FULL)], w_in[k]).astype(BF16)
        core_copy(i).start()

    def stage_c(i, half):
        core_copy(i).wait_recv()

        def add(k, carry):
            quarter = k % 4
            here = mine(quarter, 0, 32)
            there = rows(i * BLOCK + ((y + quarter) % 4) * 32, 32)
            part[i, here] = (part[i, here].astype(F32) + core_in[there].astype(F32)).astype(BF16)
            return carry

        lax.fori_loop(1, 4, add, 0)
        y_raw_copy(i, 0, 2, 0, y_up).start()
        y_raw_copy(i, 1, 2, 1, y_down).start()
        y_raw_copy(i, 2, 1, 1, y_up).start()
        y_raw_copy(i, 3, 3, 0, y_down).start()
        lax.fori_loop(4, 5, add, 0)

    def stage_y1(i, half):
        await_bytes(wide_rows(2 * ROW), y1_r.at[i])
        for side, quarter, device in ((0, 1, y_up), (1, 3, y_down)):
            y_raw[i, side] = (y_raw[i, side].astype(F32) + part[i, mine(quarter, side, ROW)].astype(F32)).astype(BF16)
            y_sum_copy(i, side, device).start()

    def stage_y2(i, half):
        await_bytes(wide_rows(4 * ROW), y2_r.at[i])
        for side, raw in ((0, 3), (1, 2)):
            total = part[i, mine(0, side, ROW)].astype(F32) + y_raw[i, raw].astype(F32) + y_sum[i, side].astype(F32)
            pair[i, side] = total.astype(BF16)
        pair_copy(i).start()

    def activate(i, total):
        gate, up, d_hidden = total[:, :HIDE], total[:, HIDE : 2 * HIDE], total[:, 2 * HIDE :]
        sigmoid = jax.nn.sigmoid(gate)
        activated = gate * sigmoid
        here = mine(0, xh, ROW)
        acts[i, here, pl.ds(0, HIDE)] = (activated * up).astype(BF16)
        acts[i, here, pl.ds(HIDE, HIDE)] = (d_hidden * up * sigmoid * (1.0 + gate * (1.0 - sigmoid))).astype(BF16)
        acts[i, here, pl.ds(2 * HIDE, HIDE)] = (d_hidden * activated).astype(BF16)

    def stage_xn(i, half):
        pair_copy(i).wait_recv()
        activate(i, pair[i, xh].astype(F32) + pair_in[i].astype(F32))

    def stage_x(i, half):
        stage_xn(i, half)
        acts_copy(i, mine(0, xh, ROW), gx_r, across).start()

    cols = (pl.ds(0, CUT), pl.ds(CUT, C - CUT))

    def side_copy(i, k):
        return copy(part.at[i, mine(k, 1 - xh, ROW)], side_in.at[i, k], dp_s.at[i], x_r.at[i], across)

    def raw_cols(i, kind, quarter, cut, device):
        where = cols[cut]
        source = part.at[i, mine(quarter, xh, ROW), where]
        return copy(source, y_raw.at[i, kind, :, where], dp_s.at[i], (y1_r if kind < 2 else y2_r).at[i], device)

    def sum_cols(i, cut, device):
        where = cols[cut]
        return copy(y_raw.at[i, cut, :, where], y_sum.at[i, cut, :, where], dp_s.at[i], y2_r.at[i], device)

    def stage_cx(i, half):
        core_copy(i).wait_recv()

        def add(k, carry):
            here = mine(k, 0, 32)
            there = rows(i * BLOCK + ((y + k) % 4) * 32, 32)
            part[i, here] = (part[i, here].astype(F32) + core_in[there].astype(F32)).astype(BF16)
            side_copy(i, k % 4).start()
            return carry

        lax.fori_loop(2, 6, add, 0)

    def stage_xa(i, half):
        await_bytes(wide_rows(4 * ROW), x_r.at[i])
        for k in (2, 3, 1, 0):
            here = mine(k, xh, ROW)
            part[i, here] = (part[i, here].astype(F32) + side_in[i, k].astype(F32)).astype(BF16)
            if k == 2:
                raw_cols(i, 0, 2, 0, y_up).start()
                raw_cols(i, 1, 2, 1, y_down).start()
            if k == 3:
                raw_cols(i, 3, 3, 0, y_down).start()
            if k == 1:
                raw_cols(i, 2, 1, 1, y_up).start()

    def stage_y1x(i, half):
        await_bytes(wide_rows(ROW), y1_r.at[i])
        for cut, quarter, device in ((0, 1, y_up), (1, 3, y_down)):
            where = cols[cut]
            term = part[i, mine(quarter, xh, ROW), where].astype(F32)
            y_raw[i, cut, :, where] = (y_raw[i, cut, :, where].astype(F32) + term).astype(BF16)
            sum_cols(i, cut, device).start()

    def stage_xxn(i, half):
        await_bytes(wide_rows(2 * ROW), y2_r.at[i])
        terms = [
            part[i, mine(0, xh, ROW), cols[cut]].astype(F32)
            + y_raw[i, raw, :, cols[cut]].astype(F32)
            + y_sum[i, cut, :, cols[cut]].astype(F32)
            for cut, raw in ((0, 3), (1, 2))
        ]
        activate(i, jnp.concatenate(terms, axis=1))

    def stage_xx(i, half):
        stage_xxn(i, half)
        acts_copy(i, mine(0, xh, ROW), gx_r, across).start()

    def g1_cols(i, way, part_no, quarter, device):
        where = (i, mine(quarter, xh, ROW), cols[way ^ part_no])
        return copy(acts.at[where], acts.at[where], dp_s.at[i], (g2_r if part_no else g1_r).at[i], device)

    def g2_cols(i, way, quarter, device):
        where = (i, mine(quarter, xh, ROW), cols[way])
        return copy(acts.at[where], acts.at[where], dp_s.at[i], g2_r.at[i], device)

    def ga_copy(i, quarter):
        return acts_copy(i, mine(quarter, xh, ROW), gx_r, across)

    def stage_ga(i, half):
        for n in range(2):
            g1_cols(i, 0, n, 0, y_up).start()
            g1_cols(i, 1, n, 0, y_down).start()
        ga_copy(i, 0).start()

    def stage_g1x(i, half):
        await_bytes(wide_rows(ROW), g1_r.at[i])
        g2_cols(i, 0, 3, y_up).start()
        g2_cols(i, 1, 1, y_down).start()

    def stage_g2x(i, half):
        await_bytes(wide_rows(2 * ROW), g2_r.at[i])
        for quarter in (3, 1, 2):
            ga_copy(i, quarter).start()

    def stage_g3x(i, half):
        await_bytes(wide_rows(4 * ROW), gx_r.at[i])
        acts_copy(i, rows(core * BLOCK, BLOCK), gc_r, sibling).start()

    def g1_copy(i, part_no, where, device):
        return acts_copy(i, where, g2_r if part_no else g1_r, device)

    def stage_g1(i, half):
        await_bytes(wide_rows(ROW), gx_r.at[i])
        g1_copy(i, 0, mine(0, 0, ROW), y_up).start()
        g1_copy(i, 0, mine(0, 1, ROW), y_down).start()
        g1_copy(i, 1, mine(0, 1, ROW), y_up).start()
        g1_copy(i, 1, mine(0, 0, ROW), y_down).start()
        acts_copy(i, mine(0, 0, 32), gc_r, sibling).start()

    def stage_g2(i, half):
        await_bytes(wide_rows(2 * ROW), g1_r.at[i])
        acts_copy(i, mine(3, 0, ROW), g2_r, y_up).start()
        acts_copy(i, mine(1, 1, ROW), g2_r, y_down).start()

    def stage_g3(i, half):
        await_bytes(wide_rows(4 * ROW), g2_r.at[i])
        for quarter in (3, 1, 2):
            acts_copy(i, mine(quarter, 0, 32), gc_r, sibling).start()

    def stage_g4(i, half):
        await_bytes(wide_rows(BLOCK), gc_r.at[i])
        output = dot(acts[i, :, pl.ds(0, HIDE)], w_out[0])
        d_tokens = dot(acts[i, :, pl.ds(HIDE, HIDE)], w_out[1]) + dot(acts[i, :, pl.ds(2 * HIDE, HIDE)], w_out[2])
        outs[i, :, pl.ds(0, FULL - 128)] = output[:, : FULL - 128].astype(BF16)
        outs[i, :, pl.ds(FULL - 128, 128)] = (output[:, FULL - 128 :] + d_tokens[:, :128]).astype(BF16)
        outs[i, :, pl.ds(FULL, FULL - 128)] = d_tokens[:, 128:].astype(BF16)

    def stage_w(i, half):
        left = toks[i, :, pl.ds(0, FULL)].T[:WIDE]
        grads[0] += dot(left, acts[i, :, pl.ds(HIDE, HIDE)])
        grads[1] += dot(left, acts[i, :, pl.ds(2 * HIDE, HIDE)])
        left = toks[i, :, pl.ds(FULL - 128, FULL)].T[EDGE:]
        grads[2] += dot(left, acts[i, :, pl.ds(0, HIDE)])

    def stage_k(i, half):
        p, hr = i % 4, i // 4
        step = 3 - p
        ahead, behind = outs.at[i, rows(half * CHAIN_ROWS, CHAIN_ROWS)], outs.at[i, rows(BLOCK + half * CHAIN_ROWS, CHAIN_ROWS)]

        @pl.when(p == 3)
        def _():
            @pl.when(hr == 0)
            def _():
                chain_copy(behind, 0, 0, 0, half, z_up).start()

            @pl.when(hr == 1)
            def _():
                chain_copy(behind, 1, 1, 0, half, z_down).start()

        @pl.when(p < 3)
        def _():
            @pl.when(p == 2)
            def _():
                await_bytes(chain_in.at[hr, 0, 0, half], k_r.at[hr, 0, half])

            @pl.when(p < 2)
            def _():
                await_bytes(toks.at[0, rows(0, 2 * CHAIN_ROWS)], k_r.at[hr, step - 1, half])

            for way, block, device in ((0, ahead, z_up), (1, behind, z_down)):
                @pl.when((step > 1) | (hr == way))
                def _():
                    block[...] = (block[...].astype(F32) + chain_in[hr, way, step - 1, half].astype(F32)).astype(BF16)

                chain_copy(block, hr, way, step, half, device).start()

    def stage_ki(hr, half):
        here = rows(half * CHAIN_ROWS, CHAIN_ROWS)
        block = outs.at[hr * 4 + 3, here]
        await_bytes(toks.at[0, rows(0, 2 * CHAIN_ROWS)], k_r.at[hr, 3, half])
        total = block[...].astype(F32) + chain_in[hr, 0, 3, half].astype(F32) + chain_in[hr, 1, 3, half].astype(F32)
        block[...] = total.astype(BF16)

        @pl.when(hr == 0)
        def _():
            first[here] = total

        @pl.when(hr == 1)
        def _():
            last_copy(half).start()

    def stage_s(i, half):
        @pl.when(i == 3)
        def _():
            await_bytes(toks.at[i, rows(0, BLOCK)], z_s.at[i])

        @pl.when(i != 3)
        def _():
            await_bytes(toks.at[i], z_s.at[i])

        await_bytes(wide_rows(30 * ROW), dp_s.at[i])

    def store(k):
        return pltpu.make_async_copy(grads.at[k], grads_hbm.at[k], store_sem.at[k])

    def stage_go(i, half):
        @pl.when(i == 0)
        def _():
            for k in range(3):
                store(k).start()

    barrier = pltpu.get_barrier_semaphore()
    peers = (sibling, y_up, y_down, across, mate, z_up, z_down)
    for device in peers:
        pl.semaphore_signal(barrier, inc=1, device_id=device, device_id_type=MESH)
    features = [
        pltpu.make_async_copy(ref, features_t.at[pl.ds(k * WIDE, WIDE)], load_sem.at[3 + k])
        for k, ref in enumerate((tokens_hbm, cotangent_hbm))
    ]
    loads = [
        pltpu.make_async_copy(ref, codes.at[k], load_sem.at[k]) for k, ref in enumerate((gate_hbm, up_hbm, down_hbm))
    ]
    for load in features + loads:
        load.start()
    for load in features:
        load.wait()
    own[...] = features_t[...].T
    pl.semaphore_wait(barrier, len(peers))

    for half in range(Z_PARTS):
        z_copy(own_half(half), 0, 1, half, z_up).start()
        z_copy(own_half(half), 0, 0, half, z_down).start()
        xl_copy(half).start()
    toks[3, rows(0, BLOCK)] = own[...]

    zeros = jnp.zeros((EDGE, HIDE), BF16)
    grads[...] = jnp.zeros_like(grads)
    loads[0].wait()
    w_gate = (codes[0].astype(F32) * gate_scale[...].reshape(1, HIDE)).astype(BF16)
    w_in[0, :WIDE] = w_gate
    w_in[0, WIDE:] = zeros
    w_out[1] = jnp.concatenate((zeros, w_gate), axis=0).T
    loads[1].wait()
    w_up = (codes[1].astype(F32) * up_scale[...].reshape(1, HIDE)).astype(BF16)
    w_in[1, :WIDE] = w_up
    w_in[1, WIDE:] = zeros
    w_out[2] = jnp.concatenate((zeros, w_up), axis=0).T
    loads[2].wait()
    w_down_t = (codes[2].astype(F32) * down_scale[...].reshape(WIDE, 1)).astype(BF16)
    w_in[2, :EDGE] = zeros
    w_in[2, EDGE:] = w_down_t
    w_out[0] = jnp.concatenate((w_down_t, zeros), axis=0).T

    stages = (
        stage_xl, stage_z, stage_m, stage_c, stage_y1, stage_y2, stage_x, stage_g1, stage_g2, stage_g3, stage_g4,
        stage_w, stage_k, stage_ki, stage_s, stage_go, stage_cx, stage_xa, stage_y1x, stage_xx, stage_xn, stage_xxn, stage_ga,
        stage_g1x, stage_g2x, stage_g3x,
    )

    steps = [KINDS.index(kind) * 32 + half * 8 + i for kind, i, half in ORDER]
    steps += [KINDS.index("GO") * 32 + 1] * (-len(steps) % 3)
    words = [sum(code << (10 * k) for k, code in enumerate(steps[n : n + 3])) for n in range(0, len(steps), 3)]

    def dispatch(low, high, kind, i, half):
        if high - low == 1:
            stages[low](i, half)
            return
        middle = (low + high) // 2

        @pl.when(kind < middle)
        def _():
            dispatch(low, middle, kind, i, half)

        @pl.when(kind >= middle)
        def _():
            dispatch(middle, high, kind, i, half)

    def step(k, word):
        dispatch(0, len(stages), word // 32 % 32, word % 8, word // 8 % 4)
        return word // 1024

    def three_steps(n, carry):
        word = jnp.int32(words[0])
        for k in range(1, len(words)):
            word = jnp.where(n == k, words[k], word)
        lax.fori_loop(0, 3, step, word)
        return carry

    lax.fori_loop(0, len(words), three_steps, 0)

    await_bytes(last_in, f_r.at[0])
    total = (first[...] + last_in[...].reshape(BLOCK, 2 * WIDE).astype(F32)).astype(BF16).T
    output_t[...] = total[:WIDE]
    d_tokens_t[...] = total[WIDE:]

    await_bytes(toks.at[pl.ds(0, 7)], k_s.at[0])
    await_bytes(last_in, f_s.at[0])
    for k in range(3):
        store(k).wait()


def settle(output_in, d_tokens_in, grads_in, output_t, d_tokens_t, grad_gate, grad_up, grad_down_t, edges, held, sems):
    pairs = [(output_in, edges.at[0], output_t), (d_tokens_in, edges.at[1], d_tokens_t)]
    pairs += [(grads_in.at[k], held.at[k], grad) for k, grad in enumerate((grad_gate, grad_up, grad_down_t))]
    loads = [pltpu.make_async_copy(a, b, sems.at[0, k]) for k, (a, b, _) in enumerate(pairs)]
    stores = [pltpu.make_async_copy(b, c, sems.at[1, k]) for k, (_, b, c) in enumerate(pairs)]
    for one in loads:
        one.start()
    for load, one in zip(loads, stores):
        load.wait()
        one.start()
    for one in stores:
        one.wait()


def local(tokens, cotangent, gate_codes, gate_scale, up_codes, up_scale, down_codes, down_scale):
    vmem = pl.BlockSpec(memory_space=pltpu.VMEM)
    dma = pltpu.SemaphoreType.DMA
    anywhere = pl.BlockSpec(memory_space=pl.ANY)
    edge = jax.ShapeDtypeStruct((WIDE, BLOCK), BF16)
    results = pl.pallas_call(
        kernel,
        out_shape=(edge, edge, jax.ShapeDtypeStruct((3, WIDE, HIDE), F32)),
        in_specs=[anywhere, anywhere, anywhere, vmem, anywhere, vmem, anywhere, vmem],
        out_specs=(vmem, vmem, anywhere),
        scratch_shapes=[
            pltpu.VMEM((2 * WIDE, BLOCK), BF16),
            pltpu.VMEM((3, WIDE, HIDE), BF16),
            pltpu.VMEM((3, WIDE, HIDE), F32),
            dma((5,)),
            dma((3,)),
            pltpu.VMEM((BLOCK, 2 * WIDE), BF16),
            pltpu.VMEM((UNITS, UNIT, 2 * WIDE), BF16),
            pltpu.VMEM((3, FULL, HIDE), BF16),
            pltpu.VMEM((3, HIDE, FULL), BF16),
            pltpu.VMEM((UNITS, UNIT, C), BF16),
            pltpu.VMEM((UNITS * BLOCK, C), BF16),
            pltpu.VMEM((UNITS, 4, ROW, C), BF16),
            pltpu.VMEM((UNITS, 2, ROW, C), BF16),
            pltpu.VMEM((UNITS, 2, ROW, C), BF16),
            pltpu.VMEM((UNITS, ROW, C), BF16),
            pltpu.VMEM((UNITS, UNIT, C), BF16),
            pltpu.VMEM((UNITS, UNIT, 2 * WIDE), BF16),
            pltpu.VMEM((2, 2, 4, CHAIN_PARTS, CHAIN_ROWS, 2 * WIDE), BF16),
            pltpu.VMEM((BLOCK, 2 * WIDE), F32),
            pltpu.VMEM((CHAIN_PARTS, CHAIN_ROWS, 2 * WIDE), BF16),
            pltpu.VMEM((UNITS, 4, ROW, C), BF16),
            dma((UNITS,)),
            dma((UNITS,)),
            dma((1,)),
            dma((1,)),
            dma((UNITS, Z_PARTS)),
            dma((Z_PARTS,)),
            *[dma((UNITS,))] * 8,
            dma((2, 4, CHAIN_PARTS)),
            dma((1,)),
        ],
        compiler_params=pltpu.CompilerParams(
            collective_id=0, has_side_effects=True, vmem_limit_bytes=64 * 1024 * 1024 - 256 * 1024
        ),
    )(
        tokens.T, cotangent.T, gate_codes, gate_scale, up_codes, up_scale, down_codes.T, down_scale.reshape(WIDE)
    )
    grad = jax.ShapeDtypeStruct((WIDE, HIDE), F32)
    output_t, d_tokens_t, grad_gate, grad_up, grad_down_t = pl.pallas_call(
        settle,
        out_shape=(edge, edge, grad, grad, grad),
        in_specs=[anywhere] * 3,
        out_specs=(anywhere,) * 5,
        scratch_shapes=[pltpu.VMEM((2, WIDE, BLOCK), BF16), pltpu.VMEM((3, WIDE, HIDE), F32), dma((2, 5))],
        compiler_params=pltpu.CompilerParams(vmem_limit_bytes=60 * 1024 * 1024),
    )(*results)
    return output_t.T, d_tokens_t.T, grad_gate, grad_up, grad_down_t.T


def solution(mesh):
    placed = (
        P("fsdp", "dp"),
        P("fsdp", "dp"),
        P("dp", "fsdp"),
        P("fsdp"),
        P("dp", "fsdp"),
        P("fsdp"),
        P("fsdp", "dp"),
        P(None, "dp"),
    )
    return jax.shard_map(
        local,
        mesh=mesh,
        in_specs=placed,
        out_specs=(
            P("fsdp", "dp"),
            P("fsdp", "dp"),
            P("dp", "fsdp"),
            P("dp", "fsdp"),
            P("fsdp", "dp"),
        ),
        check_vma=False,
    )
```

```python
import functools

import jax
import jax.numpy as jnp
from jax import lax
from jax.experimental import pallas as pl
from jax.experimental.pallas import tpu as pltpu
from jax.sharding import PartitionSpec as P

MESH = pl.DeviceIdType.MESH
BF16 = jnp.bfloat16
F32 = jnp.float32

BLOCK = 128
UNIT = 256
UNITS = 8
WIDE = 448
HIDE = 896
FULL = 512
C = 3 * HIDE
ROW = 16
Z_PARTS = 4
Z_ROWS = BLOCK // Z_PARTS
CHAIN_PARTS = 2
CHAIN_ROWS = BLOCK // CHAIN_PARTS
CUT = 11 * 128
EDGE = FULL - WIDE

ORDER = (
    ("Z", 0, 0), ("Z", 0, 1), ("Z", 0, 2), ("Z", 0, 3), ("M", 0, 0), ("Z", 1, 0), ("Z", 1, 1), ("Z", 1, 2),
    ("CX", 0, 0), ("Z", 1, 3), ("M", 1, 0), ("Z", 2, 0), ("Z", 2, 1), ("Z", 2, 2), ("C", 1, 0), ("Z", 2, 3),
    ("XL", 0, 0), ("M", 2, 0), ("Z", 3, 0), ("Z", 3, 1), ("Y1", 1, 0), ("Z", 3, 2), ("XL", 0, 1), ("XL", 0, 2),
    ("C", 2, 0), ("Z", 3, 3), ("M", 3, 0), ("XL", 0, 3), ("Z", 4, 0), ("Z", 7, 0), ("Y2", 1, 0), ("Z", 4, 1),
    ("Z", 4, 2), ("C", 3, 0), ("Z", 7, 1), ("Z", 7, 2), ("Z", 4, 3), ("M", 4, 0), ("Z", 7, 3), ("XA", 0, 0),
    ("Z", 5, 0), ("M", 7, 0), ("Z", 5, 1), ("Y1", 3, 0), ("CX", 4, 0), ("Z", 5, 2), ("Z", 5, 3), ("Z", 6, 0),
    ("C", 7, 0), ("Z", 6, 1), ("Y1", 2, 0), ("Z", 6, 2), ("Z", 6, 3), ("M", 6, 0), ("Y2", 3, 0), ("Y1", 7, 0),
    ("C", 6, 0), ("Y2", 2, 0), ("Y2", 7, 0), ("XN", 3, 0), ("GA", 3, 0), ("M", 5, 0), ("Y1", 6, 0),
    ("X", 1, 0), ("G1X", 3, 0), ("X", 2, 0), ("C", 5, 0), ("XN", 7, 0), ("Y2", 6, 0), ("G2X", 3, 0),
    ("GA", 7, 0), ("Y1", 5, 0), ("G1X", 7, 0), ("G1", 2, 0), ("XN", 6, 0), ("Y2", 5, 0), ("G3X", 3, 0),
    ("G2X", 7, 0), ("G2", 2, 0), ("GA", 6, 0), ("G4", 3, 0), ("XA", 4, 0), ("K", 3, 0), ("K", 3, 1),
    ("G3", 2, 0), ("X", 5, 0), ("G1X", 6, 0), ("G1", 1, 0), ("G4", 2, 0), ("K", 2, 0), ("G2X", 6, 0),
    ("G3X", 7, 0), ("G2", 1, 0), ("K", 2, 1), ("Y1X", 4, 0), ("G4", 7, 0), ("Y1X", 0, 0), ("K", 7, 0),
    ("G1", 5, 0), ("G3", 1, 0), ("K", 7, 1), ("XX", 4, 0), ("W", 3, 0), ("G4", 1, 0), ("K", 1, 0),
    ("G2", 5, 0), ("G3X", 6, 0), ("XX", 0, 0), ("G1", 4, 0), ("K", 1, 1), ("G4", 6, 0), ("K", 6, 0),
    ("G3", 5, 0), ("G2", 4, 0), ("K", 6, 1), ("W", 1, 0), ("G1", 0, 0), ("G4", 5, 0), ("K", 5, 0),
    ("G3", 4, 0), ("W", 5, 0), ("G2", 0, 0), ("K", 5, 1), ("G4", 4, 0), ("K", 4, 0), ("G3", 0, 0), ("K", 4, 1),
    ("W", 7, 0), ("G4", 0, 0), ("KI", 1, 0), ("K", 0, 0), ("K", 0, 1), ("KI", 1, 1), ("W", 6, 0), ("W", 2, 0),
    ("W", 4, 0), ("W", 0, 0), ("GO", 0, 0), ("S", 7, 0), ("S", 6, 0), ("S", 5, 0), ("S", 4, 0), ("S", 3, 0),
    ("S", 2, 0), ("S", 1, 0), ("S", 0, 0), ("KI", 0, 0), ("KI", 0, 1),
)
KINDS = ("XL", "Z", "M", "C", "Y1", "Y2", "X", "G1", "G2", "G3", "G4", "W", "K", "KI", "S", "GO", "CX", "XA", "Y1X", "XX", "XN", "XXN", "GA", "G1X", "G2X", "G3X")


def dot(left, right):
    return jnp.dot(left, right, preferred_element_type=F32)


def kernel(
    tokens_hbm, cotangent_hbm, gate_hbm, gate_scale, up_hbm, up_scale, down_hbm, down_scale,
    output_t, d_tokens_t, grads_hbm,
    features_t, codes, grads, load_sem, store_sem, own, toks, w_in, w_out, part, core_in, y_raw, y_sum, pair, pair_in, acts, outs, chain_in, first, last_in, side_in,
    z_s, dp_s, k_s, f_s,
    z_r, xl_r, c_r, y1_r, y2_r, x_r, gx_r, g1_r, g2_r, gc_r, k_r, f_r,
):
    dp, fs = lax.axis_index("dp"), lax.axis_index("fsdp")
    y, xh, core = dp // 4, (dp // 2) % 2, dp % 2
    xl, z = fs // 8, fs % 8

    def at(y, xh, core, xl, z):
        return (y * 4 + xh * 2 + core, xl * 8 + z)

    sibling = at(y, xh, 1 - core, xl, z)
    y_up, y_down = at((y + 1) % 4, xh, core, xl, z), at((y + 3) % 4, xh, core, xl, z)
    across = at(y, 1 - xh, core, xl, z)
    mate = at(y, xh, core, 1 - xl, z)
    z_up, z_down = at(y, xh, core, xl, (z + 1) % 8), at(y, xh, core, xl, (z + 7) % 8)

    def copy(src, dst, send, recv, device):
        return pltpu.make_async_remote_copy(
            src_ref=src, dst_ref=dst, send_sem=send, recv_sem=recv, device_id=device, device_id_type=MESH
        )

    def rows(start, size):
        return pl.ds(pl.multiple_of(start, ROW), size)

    def mine(quarter, half, size):
        return rows(core * BLOCK + ((y + quarter) % 4) * 32 + half * ROW, size)

    def await_bytes(ref, semaphore):
        pltpu.make_async_copy(ref, ref, semaphore).wait()

    def wide_rows(count):
        return core_in.at[rows(0, count)]

    def z_copy(src, unit, side, half, device):
        dst = toks.at[unit, rows(side * BLOCK + half * Z_ROWS, Z_ROWS)]
        return copy(src, dst, z_s.at[unit], z_r.at[unit, half], device)

    def xl_copy(half):
        return copy(own_half(half), toks.at[7, rows(half * Z_ROWS, Z_ROWS)], z_s.at[7], xl_r.at[half], mate)

    def own_half(half):
        return own.at[rows(half * Z_ROWS, Z_ROWS)]

    def core_copy(i):
        source = part.at[i, rows((1 - core) * BLOCK, BLOCK)]
        return copy(source, core_in.at[rows(i * BLOCK, BLOCK)], dp_s.at[i], c_r.at[i], sibling)

    def y_raw_copy(i, kind, quarter, half, device):
        landed = (y1_r if kind < 2 else y2_r).at[i]
        return copy(part.at[i, mine(quarter, half, ROW)], y_raw.at[i, kind], dp_s.at[i], landed, device)

    def y_sum_copy(i, side, device):
        return copy(y_raw.at[i, side], y_sum.at[i, side], dp_s.at[i], y2_r.at[i], device)

    def pair_copy(i):
        return copy(pair.at[i, 1 - xh], pair_in.at[i], dp_s.at[i], x_r.at[i], across)

    def acts_copy(i, where, landed, device):
        return copy(acts.at[i, where], acts.at[i, where], dp_s.at[i], landed.at[i], device)

    def chain_copy(src, hr, way, step, half, device):
        return copy(src, chain_in.at[hr, way, step, half], k_s.at[0], k_r.at[hr, step, half], device)

    def last_copy(half):
        return copy(outs.at[7, rows(half * CHAIN_ROWS, CHAIN_ROWS)], last_in.at[half], f_s.at[0], f_r.at[0], mate)

    def stage_xl(i, half):
        xl_copy(half).wait_recv()
        source = toks.at[7, rows(half * Z_ROWS, Z_ROWS)]
        z_copy(source, 4, 1, half, z_up).start()
        z_copy(source, 4, 0, half, z_down).start()

    def stage_z(i, half):
        p, hr = i % 4, i // 4
        low = toks.at[i, rows(BLOCK + half * Z_ROWS, Z_ROWS)]
        high = toks.at[i, rows(half * Z_ROWS, Z_ROWS)]

        @pl.when(p < 3)
        def _():
            await_bytes(toks.at[i, rows(0, 2 * Z_ROWS)], z_r.at[i, half])

        @pl.when(p == 3)
        def _():
            await_bytes(toks.at[i, rows(BLOCK, Z_ROWS)], z_r.at[i, half])

        @pl.when(p * 4 + hr * 2 < 10)
        def _():
            z_copy(low, i + 1, 1, half, z_up).start()

        @pl.when(p < 2)
        def _():
            z_copy(high, i + 1, 0, half, z_down).start()

        @pl.when(i == 3)
        def _():
            z_copy(low, 7, 1, half, mate).start()

    def stage_m(i, half):
        for k, start in enumerate((0, 0, FULL - 128)):
            part[i, :, pl.ds(k * HIDE, HIDE)] = dot(toks[i, :, pl.ds(start, FULL)], w_in[k]).astype(BF16)
        core_copy(i).start()

    def stage_c(i, half):
        core_copy(i).wait_recv()

        def add(k, carry):
            quarter = k % 4
            here = mine(quarter, 0, 32)
            there = rows(i * BLOCK + ((y + quarter) % 4) * 32, 32)
            part[i, here] = (part[i, here].astype(F32) + core_in[there].astype(F32)).astype(BF16)
            return carry

        lax.fori_loop(1, 4, add, 0)
        y_raw_copy(i, 0, 2, 0, y_up).start()
        y_raw_copy(i, 1, 2, 1, y_down).start()
        y_raw_copy(i, 2, 1, 1, y_up).start()
        y_raw_copy(i, 3, 3, 0, y_down).start()
        lax.fori_loop(4, 5, add, 0)

    def stage_y1(i, half):
        await_bytes(wide_rows(2 * ROW), y1_r.at[i])
        for side, quarter, device in ((0, 1, y_up), (1, 3, y_down)):
            y_raw[i, side] = (y_raw[i, side].astype(F32) + part[i, mine(quarter, side, ROW)].astype(F32)).astype(BF16)
            y_sum_copy(i, side, device).start()

    def stage_y2(i, half):
        await_bytes(wide_rows(4 * ROW), y2_r.at[i])
        for side, raw in ((0, 3), (1, 2)):
            total = part[i, mine(0, side, ROW)].astype(F32) + y_raw[i, raw].astype(F32) + y_sum[i, side].astype(F32)
            pair[i, side] = total.astype(BF16)
        pair_copy(i).start()

    def activate(i, total):
        gate, up, d_hidden = total[:, :HIDE], total[:, HIDE : 2 * HIDE], total[:, 2 * HIDE :]
        sigmoid = jax.nn.sigmoid(gate)
        activated = gate * sigmoid
        here = mine(0, xh, ROW)
        acts[i, here, pl.ds(0, HIDE)] = (activated * up).astype(BF16)
        acts[i, here, pl.ds(HIDE, HIDE)] = (d_hidden * up * sigmoid * (1.0 + gate * (1.0 - sigmoid))).astype(BF16)
        acts[i, here, pl.ds(2 * HIDE, HIDE)] = (d_hidden * activated).astype(BF16)

    def stage_xn(i, half):
        pair_copy(i).wait_recv()
        activate(i, pair[i, xh].astype(F32) + pair_in[i].astype(F32))

    def stage_x(i, half):
        stage_xn(i, half)
        acts_copy(i, mine(0, xh, ROW), gx_r, across).start()

    cols = (pl.ds(0, CUT), pl.ds(CUT, C - CUT))

    def side_copy(i, k):
        return copy(part.at[i, mine(k, 1 - xh, ROW)], side_in.at[i, k], dp_s.at[i], x_r.at[i], across)

    def raw_cols(i, kind, quarter, cut, device):
        where = cols[cut]
        source = part.at[i, mine(quarter, xh, ROW), where]
        return copy(source, y_raw.at[i, kind, :, where], dp_s.at[i], (y1_r if kind < 2 else y2_r).at[i], device)

    def sum_cols(i, cut, device):
        where = cols[cut]
        return copy(y_raw.at[i, cut, :, where], y_sum.at[i, cut, :, where], dp_s.at[i], y2_r.at[i], device)

    def stage_cx(i, half):
        core_copy(i).wait_recv()

        def add(k, carry):
            here = mine(k, 0, 32)
            there = rows(i * BLOCK + ((y + k) % 4) * 32, 32)
            part[i, here] = (part[i, here].astype(F32) + core_in[there].astype(F32)).astype(BF16)
            side_copy(i, k % 4).start()
            return carry

        lax.fori_loop(2, 6, add, 0)

    def stage_xa(i, half):
        await_bytes(wide_rows(4 * ROW), x_r.at[i])
        for k in (2, 3, 1, 0):
            here = mine(k, xh, ROW)
            part[i, here] = (part[i, here].astype(F32) + side_in[i, k].astype(F32)).astype(BF16)
            if k == 2:
                raw_cols(i, 0, 2, 0, y_up).start()
                raw_cols(i, 1, 2, 1, y_down).start()
            if k == 3:
                raw_cols(i, 3, 3, 0, y_down).start()
            if k == 1:
                raw_cols(i, 2, 1, 1, y_up).start()

    def stage_y1x(i, half):
        await_bytes(wide_rows(ROW), y1_r.at[i])
        for cut, quarter, device in ((0, 1, y_up), (1, 3, y_down)):
            where = cols[cut]
            term = part[i, mine(quarter, xh, ROW), where].astype(F32)
            y_raw[i, cut, :, where] = (y_raw[i, cut, :, where].astype(F32) + term).astype(BF16)
            sum_cols(i, cut, device).start()

    def stage_xxn(i, half):
        await_bytes(wide_rows(2 * ROW), y2_r.at[i])
        terms = [
            part[i, mine(0, xh, ROW), cols[cut]].astype(F32)
            + y_raw[i, raw, :, cols[cut]].astype(F32)
            + y_sum[i, cut, :, cols[cut]].astype(F32)
            for cut, raw in ((0, 3), (1, 2))
        ]
        activate(i, jnp.concatenate(terms, axis=1))

    def stage_xx(i, half):
        stage_xxn(i, half)
        acts_copy(i, mine(0, xh, ROW), gx_r, across).start()

    def g1_cols(i, way, part_no, quarter, device):
        where = (i, mine(quarter, xh, ROW), cols[way ^ part_no])
        return copy(acts.at[where], acts.at[where], dp_s.at[i], (g2_r if part_no else g1_r).at[i], device)

    def g2_cols(i, way, quarter, device):
        where = (i, mine(quarter, xh, ROW), cols[way])
        return copy(acts.at[where], acts.at[where], dp_s.at[i], g2_r.at[i], device)

    def ga_copy(i, quarter):
        return acts_copy(i, mine(quarter, xh, ROW), gx_r, across)

    def stage_ga(i, half):
        for n in range(2):
            g1_cols(i, 0, n, 0, y_up).start()
            g1_cols(i, 1, n, 0, y_down).start()
        ga_copy(i, 0).start()

    def stage_g1x(i, half):
        await_bytes(wide_rows(ROW), g1_r.at[i])
        g2_cols(i, 0, 3, y_up).start()
        g2_cols(i, 1, 1, y_down).start()

    def stage_g2x(i, half):
        await_bytes(wide_rows(2 * ROW), g2_r.at[i])
        for quarter in (3, 1, 2):
            ga_copy(i, quarter).start()

    def stage_g3x(i, half):
        await_bytes(wide_rows(4 * ROW), gx_r.at[i])
        acts_copy(i, rows(core * BLOCK, BLOCK), gc_r, sibling).start()

    def g1_copy(i, part_no, where, device):
        return acts_copy(i, where, g2_r if part_no else g1_r, device)

    def stage_g1(i, half):
        await_bytes(wide_rows(ROW), gx_r.at[i])
        g1_copy(i, 0, mine(0, 0, ROW), y_up).start()
        g1_copy(i, 0, mine(0, 1, ROW), y_down).start()
        g1_copy(i, 1, mine(0, 1, ROW), y_up).start()
        g1_copy(i, 1, mine(0, 0, ROW), y_down).start()
        acts_copy(i, mine(0, 0, 32), gc_r, sibling).start()

    def stage_g2(i, half):
        await_bytes(wide_rows(2 * ROW), g1_r.at[i])
        acts_copy(i, mine(3, 0, ROW), g2_r, y_up).start()
        acts_copy(i, mine(1, 1, ROW), g2_r, y_down).start()

    def stage_g3(i, half):
        await_bytes(wide_rows(4 * ROW), g2_r.at[i])
        for quarter in (3, 1, 2):
            acts_copy(i, mine(quarter, 0, 32), gc_r, sibling).start()

    def stage_g4(i, half):
        await_bytes(wide_rows(BLOCK), gc_r.at[i])
        output = dot(acts[i, :, pl.ds(0, HIDE)], w_out[0])
        d_tokens = dot(acts[i, :, pl.ds(HIDE, HIDE)], w_out[1]) + dot(acts[i, :, pl.ds(2 * HIDE, HIDE)], w_out[2])
        outs[i, :, pl.ds(0, FULL - 128)] = output[:, : FULL - 128].astype(BF16)
        outs[i, :, pl.ds(FULL - 128, 128)] = (output[:, FULL - 128 :] + d_tokens[:, :128]).astype(BF16)
        outs[i, :, pl.ds(FULL, FULL - 128)] = d_tokens[:, 128:].astype(BF16)

    def stage_w(i, half):
        left = toks[i, :, pl.ds(0, FULL)].T[:WIDE]
        grads[0] += dot(left, acts[i, :, pl.ds(HIDE, HIDE)])
        grads[1] += dot(left, acts[i, :, pl.ds(2 * HIDE, HIDE)])
        left = toks[i, :, pl.ds(FULL - 128, FULL)].T[EDGE:]
        grads[2] += dot(left, acts[i, :, pl.ds(0, HIDE)])

    def stage_k(i, half):
        p, hr = i % 4, i // 4
        step = 3 - p
        ahead, behind = outs.at[i, rows(half * CHAIN_ROWS, CHAIN_ROWS)], outs.at[i, rows(BLOCK + half * CHAIN_ROWS, CHAIN_ROWS)]

        @pl.when(p == 3)
        def _():
            @pl.when(hr == 0)
            def _():
                chain_copy(behind, 0, 0, 0, half, z_up).start()

            @pl.when(hr == 1)
            def _():
                chain_copy(behind, 1, 1, 0, half, z_down).start()

        @pl.when(p < 3)
        def _():
            @pl.when(p == 2)
            def _():
                await_bytes(chain_in.at[hr, 0, 0, half], k_r.at[hr, 0, half])

            @pl.when(p < 2)
            def _():
                await_bytes(toks.at[0, rows(0, 2 * CHAIN_ROWS)], k_r.at[hr, step - 1, half])

            for way, block, device in ((0, ahead, z_up), (1, behind, z_down)):
                @pl.when((step > 1) | (hr == way))
                def _():
                    block[...] = (block[...].astype(F32) + chain_in[hr, way, step - 1, half].astype(F32)).astype(BF16)

                chain_copy(block, hr, way, step, half, device).start()

    def stage_ki(hr, half):
        here = rows(half * CHAIN_ROWS, CHAIN_ROWS)
        block = outs.at[hr * 4 + 3, here]
        await_bytes(toks.at[0, rows(0, 2 * CHAIN_ROWS)], k_r.at[hr, 3, half])
        total = block[...].astype(F32) + chain_in[hr, 0, 3, half].astype(F32) + chain_in[hr, 1, 3, half].astype(F32)
        block[...] = total.astype(BF16)

        @pl.when(hr == 0)
        def _():
            first[here] = total

        @pl.when(hr == 1)
        def _():
            last_copy(half).start()

    def stage_s(i, half):
        @pl.when(i == 3)
        def _():
            await_bytes(toks.at[i, rows(0, BLOCK)], z_s.at[i])

        @pl.when(i != 3)
        def _():
            await_bytes(toks.at[i], z_s.at[i])

        await_bytes(wide_rows(30 * ROW), dp_s.at[i])

    def store(k):
        return pltpu.make_async_copy(grads.at[k], grads_hbm.at[k], store_sem.at[k])

    def stage_go(i, half):
        @pl.when(i == 0)
        def _():
            for k in range(3):
                store(k).start()

    barrier = pltpu.get_barrier_semaphore()
    peers = (sibling, y_up, y_down, across, mate, z_up, z_down)
    for device in peers:
        pl.semaphore_signal(barrier, inc=1, device_id=device, device_id_type=MESH)
    features = [
        pltpu.make_async_copy(ref, features_t.at[pl.ds(k * WIDE, WIDE)], load_sem.at[3 + k])
        for k, ref in enumerate((tokens_hbm, cotangent_hbm))
    ]
    loads = [
        pltpu.make_async_copy(ref, codes.at[k], load_sem.at[k]) for k, ref in enumerate((gate_hbm, up_hbm, down_hbm))
    ]
    for load in features + loads:
        load.start()
    for load in features:
        load.wait()
    own[...] = features_t[...].T
    pl.semaphore_wait(barrier, len(peers))

    for half in range(Z_PARTS):
        z_copy(own_half(half), 0, 1, half, z_up).start()
        z_copy(own_half(half), 0, 0, half, z_down).start()
        xl_copy(half).start()
    toks[3, rows(0, BLOCK)] = own[...]

    zeros = jnp.zeros((EDGE, HIDE), BF16)
    grads[...] = jnp.zeros_like(grads)
    loads[0].wait()
    w_gate = (codes[0].astype(F32) * gate_scale[...].reshape(1, HIDE)).astype(BF16)
    w_in[0, :WIDE] = w_gate
    w_in[0, WIDE:] = zeros
    w_out[1] = jnp.concatenate((zeros, w_gate), axis=0).T
    loads[1].wait()
    w_up = (codes[1].astype(F32) * up_scale[...].reshape(1, HIDE)).astype(BF16)
    w_in[1, :WIDE] = w_up
    w_in[1, WIDE:] = zeros
    w_out[2] = jnp.concatenate((zeros, w_up), axis=0).T
    loads[2].wait()
    w_down_t = (codes[2].astype(F32) * down_scale[...].reshape(WIDE, 1)).astype(BF16)
    w_in[2, :EDGE] = zeros
    w_in[2, EDGE:] = w_down_t
    w_out[0] = jnp.concatenate((w_down_t, zeros), axis=0).T

    stages = (
        stage_xl, stage_z, stage_m, stage_c, stage_y1, stage_y2, stage_x, stage_g1, stage_g2, stage_g3, stage_g4,
        stage_w, stage_k, stage_ki, stage_s, stage_go, stage_cx, stage_xa, stage_y1x, stage_xx, stage_xn, stage_xxn, stage_ga,
        stage_g1x, stage_g2x, stage_g3x,
    )

    for kind, i, half in ORDER:
        stages[KINDS.index(kind)](i, half)

    await_bytes(last_in, f_r.at[0])
    total = (first[...] + last_in[...].reshape(BLOCK, 2 * WIDE).astype(F32)).astype(BF16).T
    output_t[...] = total[:WIDE]
    d_tokens_t[...] = total[WIDE:]

    await_bytes(toks.at[pl.ds(0, 7)], k_s.at[0])
    await_bytes(last_in, f_s.at[0])
    for k in range(3):
        store(k).wait()


def settle(output_in, d_tokens_in, grads_in, output_t, d_tokens_t, grad_gate, grad_up, grad_down_t, edges, held, sems):
    pairs = [(output_in, edges.at[0], output_t), (d_tokens_in, edges.at[1], d_tokens_t)]
    pairs += [(grads_in.at[k], held.at[k], grad) for k, grad in enumerate((grad_gate, grad_up, grad_down_t))]
    loads = [pltpu.make_async_copy(a, b, sems.at[0, k]) for k, (a, b, _) in enumerate(pairs)]
    stores = [pltpu.make_async_copy(b, c, sems.at[1, k]) for k, (_, b, c) in enumerate(pairs)]
    for one in loads:
        one.start()
    for load, one in zip(loads, stores):
        load.wait()
        one.start()
    for one in stores:
        one.wait()


def local(tokens, cotangent, gate_codes, gate_scale, up_codes, up_scale, down_codes, down_scale):
    vmem = pl.BlockSpec(memory_space=pltpu.VMEM)
    dma = pltpu.SemaphoreType.DMA
    anywhere = pl.BlockSpec(memory_space=pl.ANY)
    edge = jax.ShapeDtypeStruct((WIDE, BLOCK), BF16)
    results = pl.pallas_call(
        kernel,
        out_shape=(edge, edge, jax.ShapeDtypeStruct((3, WIDE, HIDE), F32)),
        in_specs=[anywhere, anywhere, anywhere, vmem, anywhere, vmem, anywhere, vmem],
        out_specs=(vmem, vmem, anywhere),
        scratch_shapes=[
            pltpu.VMEM((2 * WIDE, BLOCK), BF16),
            pltpu.VMEM((3, WIDE, HIDE), BF16),
            pltpu.VMEM((3, WIDE, HIDE), F32),
            dma((5,)),
            dma((3,)),
            pltpu.VMEM((BLOCK, 2 * WIDE), BF16),
            pltpu.VMEM((UNITS, UNIT, 2 * WIDE), BF16),
            pltpu.VMEM((3, FULL, HIDE), BF16),
            pltpu.VMEM((3, HIDE, FULL), BF16),
            pltpu.VMEM((UNITS, UNIT, C), BF16),
            pltpu.VMEM((UNITS * BLOCK, C), BF16),
            pltpu.VMEM((UNITS, 4, ROW, C), BF16),
            pltpu.VMEM((UNITS, 2, ROW, C), BF16),
            pltpu.VMEM((UNITS, 2, ROW, C), BF16),
            pltpu.VMEM((UNITS, ROW, C), BF16),
            pltpu.VMEM((UNITS, UNIT, C), BF16),
            pltpu.VMEM((UNITS, UNIT, 2 * WIDE), BF16),
            pltpu.VMEM((2, 2, 4, CHAIN_PARTS, CHAIN_ROWS, 2 * WIDE), BF16),
            pltpu.VMEM((BLOCK, 2 * WIDE), F32),
            pltpu.VMEM((CHAIN_PARTS, CHAIN_ROWS, 2 * WIDE), BF16),
            pltpu.VMEM((UNITS, 4, ROW, C), BF16),
            dma((UNITS,)),
            dma((UNITS,)),
            dma((1,)),
            dma((1,)),
            dma((UNITS, Z_PARTS)),
            dma((Z_PARTS,)),
            *[dma((UNITS,))] * 8,
            dma((2, 4, CHAIN_PARTS)),
            dma((1,)),
        ],
        compiler_params=pltpu.CompilerParams(
            collective_id=0, has_side_effects=True, vmem_limit_bytes=64 * 1024 * 1024 - 256 * 1024
        ),
    )(
        tokens.T, cotangent.T, gate_codes, gate_scale, up_codes, up_scale, down_codes.T, down_scale.reshape(WIDE)
    )
    grad = jax.ShapeDtypeStruct((WIDE, HIDE), F32)
    output_t, d_tokens_t, grad_gate, grad_up, grad_down_t = pl.pallas_call(
        settle,
        out_shape=(edge, edge, grad, grad, grad),
        in_specs=[anywhere] * 3,
        out_specs=(anywhere,) * 5,
        scratch_shapes=[pltpu.VMEM((2, WIDE, BLOCK), BF16), pltpu.VMEM((3, WIDE, HIDE), F32), dma((2, 5))],
        compiler_params=pltpu.CompilerParams(vmem_limit_bytes=60 * 1024 * 1024),
    )(*results)
    return output_t.T, d_tokens_t.T, grad_gate, grad_up, grad_down_t.T


def solution(mesh):
    placed = (
        P("fsdp", "dp"),
        P("fsdp", "dp"),
        P("dp", "fsdp"),
        P("fsdp"),
        P("dp", "fsdp"),
        P("fsdp"),
        P("fsdp", "dp"),
        P(None, "dp"),
    )
    return jax.shard_map(
        local,
        mesh=mesh,
        in_specs=placed,
        out_specs=(
            P("fsdp", "dp"),
            P("fsdp", "dp"),
            P("dp", "fsdp"),
            P("dp", "fsdp"),
            P("fsdp", "dp"),
        ),
        check_vma=False,
    )
```
